32 devices in a mesh: col: 8 (over z, y), row: 4 (over x, core).
Axes of the slice: x: 2, y: 2, z: 4, core: 2. Of those that a mesh axis runs over, the one named last changes fastest.
Arguments:
- u_factors: bfloat16 [2, 64, 256, 64, 128], P(None, 'row', None, 'col'), may hold values from -0.09375 to 0.09375
- v_factors: bfloat16 [2, 64, 256, 64, 128], P(None, 'row', None, 'col'), may hold values from -0.375 to 0.375
- ranks: int32 [2, 64, 64], P(None, 'row', 'col'), may hold values from 8 to 64
- model_init: float32 [2, 16384, 256], P(None, ('col', 'row')), may hold values from -6 to 6
- observed: float32 [2, 16384, 256], P(None, ('row', 'col')), may hold values from -6 to 6
- step: float32 [2], replicated, may hold values from 0.1 to 0.4
Outputs:
- model: float32 [2, 16384, 256], P(None, ('col', 'row'))
- misfit: float32 [2, 16384, 256], P(None, ('row', 'col'))
The draws below stay inside these ranges and needn't reach their ends.
Inputs may be any that keep to these rules, and one draw needn't show every extreme that they name: `ranks`: columns of a factor beyond its tile's rank do not count.
All inputs are finite; a program needn't handle non-finite values.
Results may differ from the reference program's by a relative error of at most 0.0085.
Values may be sent and summed in bfloat16 or wider, within the bound.
No kernel may reach another device: no remote copies, remote signals or barrier semaphores. Data moves between devices by JAX's collectives and lax.ppermute only.
A program may use at most 192 MiB of HBM per device.

```python
import math
import jax
import jax.numpy as jnp
from jax import lax

ORDER = 16384
TILE = 256
RMAX = 64
RHS = 128
FREQS = 2
ITERS = 2
TILES = 64


def touch_ends(drawn, rng, least, high):
    longest = drawn.shape.index(max(drawn.shape))
    spots = []
    for shift in (0, 1):
        where = [jax.random.randint(jax.random.fold_in(rng, axis), (), 0, length) for axis, length in enumerate(drawn.shape)]
        where[longest] = (where[longest] + shift) % drawn.shape[longest]
        spots.append(tuple(where))
    return drawn.at[spots[0]].set(least).at[spots[1]].set(high)


def block_levels(own_key, dims, cuts, smallest, high):
    loudness, own = 1.0, jax.random.fold_in(own_key, 6)
    for axis_at, blocks in cuts:
        steps = jnp.exp(jax.random.uniform(jax.random.fold_in(own, axis_at), (blocks,), jnp.float32, smallest / len(cuts), high / len(cuts)))
        loudness = loudness * jnp.repeat(steps, dims[axis_at] // blocks).reshape([-1 if axis == axis_at else 1 for axis in range(len(dims))])
    return loudness


def noise(rng, shape, scale, reach, cuts=(), kind=jnp.bfloat16):
    result = jax.random.normal(rng, shape, jnp.float32) * scale
    if len(cuts) > 0:
        result = block_levels(rng, shape, cuts, -0.22, 0.18) * result
    return jnp.clip(result, min=-reach, max=reach).astype(kind)


def setup_inputs(seed: int = 0) -> dict:
    arg_keys = jax.random.split(jax.random.key(seed), 7)
    u_factors = noise(arg_keys[0], (FREQS, TILES, TILE, TILES, 2 * RMAX), (TILES * RMAX) ** -0.5, 0.09375, ((1, 4), (3, 8)))
    v_factors = noise(arg_keys[1], (FREQS, TILES, TILE, TILES, 2 * RMAX), TILE ** -0.5, 0.375, ((1, 4), (3, 8)))
    ranks = touch_ends(jax.random.randint(arg_keys[2], (FREQS, TILES, TILES), RMAX // 8, RMAX + 1), jax.random.fold_in(arg_keys[2], 1), RMAX // 8, RMAX).astype(jnp.int32)
    model_init = noise(arg_keys[3], (FREQS, ORDER, 2 * RHS), 1.0, 6.0, ((1, 32),), jnp.float32)
    observed = noise(arg_keys[4], (FREQS, ORDER, 2 * RHS), 1.0, 6.0, ((1, 32),), jnp.float32)
    step = jnp.clip(jnp.exp(jax.random.uniform(arg_keys[5], (FREQS,), jnp.float32, math.log(0.1), math.log(0.4))), 0.1, 0.4)
    return dict(u_factors=u_factors, v_factors=v_factors, ranks=ranks, model_init=model_init, observed=observed, step=step)


def split_product(product, rank_mask):
    real = product[..., :RMAX, :RHS] + product[..., RMAX:, RHS:]
    imaginary = product[..., :RMAX, RHS:] - product[..., RMAX:, :RHS]
    weights = rank_mask[..., None]
    return jnp.concatenate([real * weights, imaginary * weights], -1).astype(jnp.bfloat16)


def expand_complex(coefficient):
    real = coefficient[..., :RHS]
    imaginary = coefficient[..., RHS:]
    upper = jnp.concatenate([real, imaginary], -1)
    lower = jnp.concatenate([-imaginary, real], -1)
    return jnp.concatenate([upper, lower], -2).astype(jnp.float32)


def reference(u_factors, v_factors, ranks, model_init, observed, step):
    rank_mask = (jnp.arange(RMAX, dtype=jnp.int32)[None, None, None, :] < ranks[..., None]).astype(jnp.float32)
    model = model_init
    misfit = model_init
    for sweep in range(ITERS):
        model_half = model.astype(jnp.bfloat16).astype(jnp.float32).reshape(FREQS, TILES, TILE, 2 * RHS)

        def forward_row(tile_row):
            left = u_factors[:, tile_row].astype(jnp.float32)
            right = v_factors[:, tile_row].astype(jnp.float32)
            product = jnp.einsum('fajk,fjal->fjkl', right, model_half)
            coefficient = split_product(product, rank_mask[:, tile_row])
            return jnp.einsum('fajk,fjkl->fal', left, expand_complex(coefficient))

        predicted = lax.map(forward_row, jnp.arange(TILES, dtype=jnp.int32))
        predicted = predicted.transpose(1, 0, 2, 3).reshape(FREQS, ORDER, 2 * RHS)
        misfit = predicted - observed
        misfit_half = misfit.astype(jnp.bfloat16).astype(jnp.float32).reshape(FREQS, TILES, TILE, 2 * RHS)

        def adjoint_row(running, tile_row):
            left = u_factors[:, tile_row].astype(jnp.float32)
            right = v_factors[:, tile_row].astype(jnp.float32)
            rows_here = lax.dynamic_index_in_dim(misfit_half, tile_row, 1, keepdims=False)
            product = jnp.einsum('fajk,fal->fjkl', left, rows_here)
            back = split_product(product, rank_mask[:, tile_row])
            return running + jnp.einsum('fajk,fjkl->fjal', right, expand_complex(back)), None

        start = jnp.zeros((FREQS, TILES, TILE, 2 * RHS), jnp.float32)
        gradient, unused = lax.scan(adjoint_row, start, jnp.arange(TILES, dtype=jnp.int32))
        model = model - step[:, None, None] * gradient.reshape(FREQS, ORDER, 2 * RHS)
    return model, misfit
```

```python
import functools

import jax
import jax.numpy as jnp
from jax import lax
from jax.experimental import pallas as pl
from jax.experimental.pallas import tpu as pltpu
from jax.sharding import PartitionSpec as P

ITERS = 2
GROUPS = 1
VMEM = 48 << 20
F32 = jnp.float32
BF16 = jnp.bfloat16
CONTRACT_LAST = (((1,), (1,)), ((), ()))


def split_product(product, rank_mask, rank_most, right_count):
    real = product[..., :rank_most, :right_count] + product[..., rank_most:, right_count:]
    imaginary = product[..., :rank_most, right_count:] - product[..., rank_most:, :right_count]
    weights = rank_mask[..., None]
    return jnp.concatenate([real * weights, imaginary * weights], -1).astype(BF16)


def expand_complex(coefficient, right_count):
    real = coefficient[..., :right_count]
    imaginary = coefficient[..., right_count:]
    upper = jnp.concatenate([real, imaginary], -1)
    lower = jnp.concatenate([-imaginary, real], -1)
    return jnp.concatenate([upper, lower], -2)


def local_plain(u_factors, v_factors, ranks, model_init, observed, step):
    frequencies = model_init.shape[0]
    rank_most = u_factors.shape[-1] // 2
    right_count = model_init.shape[-1] // 2
    tile_size = u_factors.shape[2]
    rows_here = u_factors.shape[1]
    cols_here = u_factors.shape[3]
    rank_mask = (
        jnp.arange(rank_most, dtype=jnp.int32)[None, None, None, :] < ranks[..., None]
    ).astype(F32)
    model = model_init
    misfit = model_init
    for sweep in range(ITERS):
        gathered = lax.all_gather(model.astype(BF16), "row", axis=1, tiled=True)
        model_tiles = gathered.reshape(frequencies, cols_here, tile_size, 2 * right_count)
        product = jnp.einsum("fiajk,fjal->fijkl", v_factors, model_tiles, preferred_element_type=F32)
        coefficient = expand_complex(split_product(product, rank_mask, rank_most, right_count), right_count)
        partial_value = jnp.einsum("fiajk,fijkl->fial", u_factors, coefficient, preferred_element_type=F32)
        partial_value = partial_value.reshape(frequencies, rows_here * tile_size, 2 * right_count)
        predicted = lax.psum_scatter(partial_value, "col", scatter_dimension=1, tiled=True)
        misfit = predicted - observed
        misfit_half = lax.all_gather(misfit.astype(BF16), "col", axis=1, tiled=True)
        misfit_tiles = misfit_half.reshape(frequencies, rows_here, tile_size, 2 * right_count)
        product = jnp.einsum("fiajk,fial->fijkl", u_factors, misfit_tiles, preferred_element_type=F32)
        back = expand_complex(split_product(product, rank_mask, rank_most, right_count), right_count)
        gradient_part = jnp.einsum("fiajk,fijkl->fjal", v_factors, back, preferred_element_type=F32)
        gradient_part = gradient_part.reshape(frequencies, cols_here * tile_size, 2 * right_count)
        gradient = lax.psum_scatter(gradient_part, "row", scatter_dimension=1, tiled=True)
        model = model - step[:, None, None] * gradient
    return (model, misfit)


def tile_columns(ref, lead, cols):
    tiles = jnp.swapaxes(ref[lead], 0, 1)
    return [tiles[j] for j in range(cols)]


def combine(product, mask):
    half_r = product.shape[0] // 2
    half_k = product.shape[1] // 2
    upper = product[:half_r]
    lower = product[half_r:]
    lane = lax.broadcasted_iota(jnp.int32, (1, 2 * half_k), 1)
    signed = jnp.where(lane < half_k, mask, -mask)
    top = upper * mask + signed * pltpu.roll(lower, half_k, 1)
    bottom = lower * mask - signed * pltpu.roll(upper, half_k, 1)
    return jnp.concatenate([top, bottom], 0).astype(BF16)


def forward_kernel(shards, u_ref, v_ref, x_ref, mask_ref, out_ref):
    rows, size, cols, width = u_ref.shape[1:]
    right = [tile_columns(v_ref, (0, i), cols) for i in range(rows)]
    coefficient = [[] for i in range(rows)]
    for j in range(cols):
        product = jnp.dot(
            x_ref[0, :, j * size : (j + 1) * size],
            jnp.concatenate([right[i][j] for i in range(rows)], 1),
            preferred_element_type=F32,
        )
        for i in range(rows):
            coefficient[i].append(
                combine(product[:, i * width : (i + 1) * width], mask_ref[0, i, :, j * width : (j + 1) * width])
            )
    for i in range(rows):
        left = jnp.concatenate(tile_columns(u_ref, (0, i), cols), 1)
        out_ref[0, 0, i * size : (i + 1) * size, :] = lax.dot_general(
            left, jnp.concatenate(coefficient[i], 1), CONTRACT_LAST, preferred_element_type=F32
        ).astype(out_ref.dtype)


def adjoint_kernel(shards, u_ref, v_ref, r_ref, mask_ref, start_ref, out_ref):
    rows, size, cols, width = u_ref.shape[1:]

    @pl.when(pl.program_id(1) == 0)
    def _():
        out_ref[...] = start_ref[...]

    adjoint_steps(u_ref, v_ref, r_ref, mask_ref, out_ref)


def adjoint_first_kernel(shards, u_ref, v_ref, r_ref, mask_ref, out_ref):
    @pl.when(pl.program_id(1) == 0)
    def _():
        out_ref[...] = jnp.zeros_like(out_ref)

    adjoint_steps(u_ref, v_ref, r_ref, mask_ref, out_ref)


def adjoint_steps(u_ref, v_ref, r_ref, mask_ref, out_ref):
    rows, size, cols, width = u_ref.shape[1:]
    back = []
    for i in range(rows):
        left = tile_columns(u_ref, (0, i), cols)
        rows_here = r_ref[0, 0, :, i * size : (i + 1) * size]
        back_row = []
        for j in range(0, cols, 2):
            product = jnp.dot(rows_here, jnp.concatenate(left[j : j + 2], 1), preferred_element_type=F32)
            for t in range(len(left[j : j + 2])):
                back_row.append(
                    combine(
                        product[:, t * width : (t + 1) * width],
                        mask_ref[0, i, :, (j + t) * width : (j + t + 1) * width],
                    )
                )
        back.append(back_row)
    right = [tile_columns(v_ref, (0, i), cols) for i in range(rows)]
    for j in range(cols):
        out_ref[0, j * size : (j + 1) * size, :] += lax.dot_general(
            jnp.concatenate([right[i][j] for i in range(rows)], 1),
            jnp.concatenate([back[i][j] for i in range(rows)], 1),
            CONTRACT_LAST,
            preferred_element_type=F32,
        )


def misfit_kernel(own_ref, fore_ref, back_ref, observed_ref, misfit_ref, half_ref):
    misfit = own_ref[0, 0] + fore_ref[0, 0].astype(F32) + back_ref[0, 0].astype(F32) - observed_ref[0]
    misfit_ref[0] = misfit
    half_ref[0, 0] = misfit.T.astype(BF16)


def half_kernel(model_ref, half_ref):
    half_ref[0] = model_ref[0].T.astype(BF16)


def model_kernel(step_ref, model_ref, own_ref, other_ref, new_ref, half_ref, *, first):
    gradient = own_ref[0] + other_ref[0].astype(F32)
    model = model_ref[0] - step_ref[first + pl.program_id(0)] * gradient
    new_ref[0] = model
    half_ref[0] = model.T.astype(BF16)


def cost(grid, rows, factors):
    size, cols, width = factors.shape[2:]
    flops = 8 * grid * rows * size * cols * width * size
    return pl.CostEstimate(flops=flops, bytes_accessed=4 * grid * rows * size * cols * width, transcendentals=0)


def forward(u, v, x, mask, shards, first, rows, dtype):
    size, cols, width = u.shape[2:]
    group, lines = x.shape[:2]
    many = shards.shape[0]
    factor = pl.BlockSpec((1, rows, size, cols, width), lambda g, d, s: (first + g, s[d], 0, 0, 0))
    return pl.pallas_call(
        forward_kernel,
        out_shape=jax.ShapeDtypeStruct((group, many, rows * size, lines), dtype),
        grid_spec=pltpu.PrefetchScalarGridSpec(
            num_scalar_prefetch=1,
            grid=(group, many),
            in_specs=[
                factor,
                factor,
                pl.BlockSpec((1, lines, cols * size), lambda g, d, s: (g, 0, 0)),
                pl.BlockSpec((1, rows, 1, cols * width), lambda g, d, s: (first + g, s[d], 0, 0)),
            ],
            out_specs=pl.BlockSpec((1, 1, rows * size, lines), lambda g, d, s: (g, d, 0, 0)),
        ),
        compiler_params=pltpu.CompilerParams(vmem_limit_bytes=VMEM),
        cost_estimate=cost(group * many, rows, u),
    )(shards, u, v, x, mask)


def adjoint(u, v, r, mask, start, shards, first, rows):
    size, cols, width = u.shape[2:]
    group, many, lines = r.shape[:3]
    factor = pl.BlockSpec((1, rows, size, cols, width), lambda g, d, s: (first + g, s[d], 0, 0, 0))
    total = pl.BlockSpec((1, cols * size, lines), lambda g, d, s: (g, 0, 0))
    return pl.pallas_call(
        adjoint_first_kernel if start is None else adjoint_kernel,
        out_shape=jax.ShapeDtypeStruct((group, cols * size, lines), F32),
        grid_spec=pltpu.PrefetchScalarGridSpec(
            num_scalar_prefetch=1,
            grid=(group, many),
            in_specs=[
                factor,
                factor,
                pl.BlockSpec((1, 1, lines, rows * size), lambda g, d, s: (g, d, 0, 0)),
                pl.BlockSpec((1, rows, 1, cols * width), lambda g, d, s: (first + g, s[d], 0, 0)),
            ]
            + ([] if start is None else [total]),
            out_specs=total,
        ),
        input_output_aliases={} if start is None else {5: 0},
        compiler_params=pltpu.CompilerParams(vmem_limit_bytes=VMEM),
        cost_estimate=cost(group * many, rows, u),
    )(shards, u, v, r, mask, *([] if start is None else [start]))


def misfit_step(own, fore, back, observed, first):
    group, many, count, lines = own.shape
    shard = pl.BlockSpec((1, 1, count, lines), lambda g: (g, 0, 0, 0))
    return pl.pallas_call(
        misfit_kernel,
        out_shape=(
            jax.ShapeDtypeStruct((group, count, lines), F32),
            jax.ShapeDtypeStruct((group, 1, lines, count), BF16),
        ),
        grid=(group,),
        in_specs=[shard, shard, shard, pl.BlockSpec((1, count, lines), lambda g: (first + g, 0, 0))],
        out_specs=(
            pl.BlockSpec((1, count, lines), lambda g: (g, 0, 0)),
            pl.BlockSpec((1, 1, lines, count), lambda g: (g, 0, 0, 0)),
        ),
        compiler_params=pltpu.CompilerParams(vmem_limit_bytes=VMEM),
    )(own, fore, back, observed)


def half_step(model, first, group):
    count, lines = model.shape[1:]
    return pl.pallas_call(
        half_kernel,
        out_shape=jax.ShapeDtypeStruct((group, lines, count), BF16),
        grid=(group,),
        in_specs=[pl.BlockSpec((1, count, lines), lambda g: (first + g, 0, 0))],
        out_specs=pl.BlockSpec((1, lines, count), lambda g: (g, 0, 0)),
        compiler_params=pltpu.CompilerParams(vmem_limit_bytes=VMEM),
    )(model)


def model_step(step, model, model_first, own, other, first):
    group, count, lines = own.shape
    block = pl.BlockSpec((1, count, lines), lambda g: (g, 0, 0))
    return pl.pallas_call(
        functools.partial(model_kernel, first=first),
        out_shape=(
            jax.ShapeDtypeStruct((group, count, lines), F32),
            jax.ShapeDtypeStruct((group, lines, count), BF16),
        ),
        grid=(group,),
        in_specs=[
            pl.BlockSpec(memory_space=pltpu.SMEM),
            pl.BlockSpec((1, count, lines), lambda g: (model_first + g, 0, 0)),
            block,
            block,
        ],
        out_specs=(block, pl.BlockSpec((1, lines, count), lambda g: (g, 0, 0))),
        compiler_params=pltpu.CompilerParams(vmem_limit_bytes=VMEM),
    )(step, model, own, other)


def ring_order(count):
    return [2 * k for k in range(count // 2)] + [2 * k + 1 for k in reversed(range(count // 2))]


class Rings:
    def __init__(self, col_count):
        order = ring_order(col_count)
        self.count = col_count
        self.order = jnp.array(order, jnp.int32)
        self.fore = [(order[k], order[(k + 1) % col_count]) for k in range(col_count)]
        self.back = [(b, a) for a, b in self.fore]
        places = [order.index(k) for k in range(col_count)]
        self.place = jnp.array(places, jnp.int32)[lax.axis_index("col")]

    def shard(self, offset):
        return self.order[(self.place + offset) % self.count]

    def shards(self, *offsets):
        return jnp.stack([self.shard(k) for k in offsets])

    def ahead(self, x):
        return lax.ppermute(x, "col", self.fore)

    def behind(self, x):
        return lax.ppermute(x, "col", self.back)


def swap_core(x):
    return lax.ppermute(x, "row", [(k, k ^ 1) for k in range(4)])


def swap_chip(x):
    return lax.ppermute(x, "row", [(k, k ^ 2) for k in range(4)])


def gather_model(half):
    across = swap_chip(half)
    beside = swap_core(half)
    corner = swap_core(across)
    row = lax.axis_index("row")
    odd = (row & 1) == 1
    upper = (row & 2) == 2
    low = [jnp.where(odd, beside, half), jnp.where(odd, half, beside)]
    high = [jnp.where(odd, corner, across), jnp.where(odd, across, corner)]
    parts = [jnp.where(upper, h, l) for h, l in zip(high, low)] + [jnp.where(upper, l, h) for h, l in zip(high, low)]
    return jnp.concatenate(parts, 2)


def scatter_gradient(total):
    group, count, lines = total.shape
    row = lax.axis_index("row")
    core = row & 1
    chip = row >> 1
    shards = total.reshape(group, 2, 2, count // 4, lines)

    def pick(x, c):
        return lax.dynamic_slice(shards, (0, x, c, 0, 0), (group, 1, 1, count // 4, lines)).reshape(
            group, count // 4, lines
        )

    far = pick(1 - chip, core) + swap_core(pick(1 - chip, 1 - core).astype(BF16)).astype(F32)
    other = swap_chip(far.astype(BF16))
    near = pick(chip, core) + swap_core(pick(chip, 1 - core).astype(BF16)).astype(F32)
    return near, other


def local_ring(u, v, ranks, model_init, observed, step, *, col_count):
    frequencies, tile_rows, size, cols, width = u.shape
    rows = tile_rows // col_count
    rings = Rings(col_count)
    far = col_count // 2
    lane = jnp.arange(width, dtype=jnp.int32) % (width // 2)
    mask = (lane < ranks[..., None]).astype(F32).reshape(frequencies, tile_rows, 1, cols * width)
    group = frequencies // GROUPS
    models, misfits = [], []
    for first in range(0, frequencies, group):
        model, model_first = model_init, first
        half = half_step(model_init, first, group)
        for sweep in range(ITERS):
            x = gather_model(half)
            cut = rows * size // 2
            part = forward(u, v, x, mask, rings.shards(far), first, rows, BF16)
            fore = rings.ahead(part[:, :, :cut])
            back = rings.behind(part[:, :, cut:])
            for k in range(far - 1, 0, -1):
                part = forward(u, v, x, mask, rings.shards(k, -k), first, rows, F32)
                up, down = part[:, :1], part[:, 1:]
                if k == far - 1:
                    up = jnp.concatenate([up[:, :, :cut] + fore.astype(F32), up[:, :, cut:]], 2)
                    down = jnp.concatenate([down[:, :, :cut], down[:, :, cut:] + back.astype(F32)], 2)
                else:
                    up = up + fore.astype(F32)
                    down = down + back.astype(F32)
                fore = rings.ahead(up.astype(BF16))
                back = rings.behind(down.astype(BF16))
            own = forward(u, v, x, mask, rings.shards(0), first, rows, F32)
            misfit, half = misfit_step(own, fore, back, observed, first)
            cut = half.shape[2] // 2
            fore = rings.ahead(half)
            back = rings.behind(half)
            total = adjoint(u, v, half, mask, None, rings.shards(0), first, rows)
            for k in range(1, far):
                arrived = [fore, back]
                if k < far - 1:
                    fore, back = rings.ahead(fore), rings.behind(back)
                else:
                    fore, back = rings.ahead(fore[:, :, :cut]), rings.behind(back[:, :, cut:])
                for shard, sign in zip(arrived, (-1, 1)):
                    total = adjoint(u, v, shard, mask, total, rings.shards(sign * k), first, rows)
            last = jnp.concatenate([fore, back], 2)
            total = adjoint(u, v, last, mask, total, rings.shards(far), first, rows)
            near, other = scatter_gradient(total)
            model, half = model_step(step, model, model_first, near, other, first)
            model_first = 0
        models.append(model)
        misfits.append(misfit)
    if GROUPS == 1:
        return (models[0], misfits[0])
    return (jnp.concatenate(models, 0), jnp.concatenate(misfits, 0))


def solution(mesh):
    col_count, row_count = mesh.shape["col"], mesh.shape["row"]

    def local(u, v, ranks, model_init, observed, step):
        if row_count == 4 and col_count % 2 == 0 and col_count >= 4 and u.shape[1] % col_count == 0:
            return local_ring(u, v, ranks, model_init, observed, step, col_count=col_count)
        return local_plain(u, v, ranks, model_init, observed, step)

    return jax.shard_map(
        local,
        mesh=mesh,
        in_specs=(
            P(None, "row", None, "col", None),
            P(None, "row", None, "col", None),
            P(None, "row", "col"),
            P(None, ("col", "row"), None),
            P(None, ("row", "col"), None),
            P(),
        ),
        out_specs=(P(None, ("col", "row"), None), P(None, ("row", "col"), None)),
        check_vma=False,
    )
```

```python
import functools

import jax
import jax.numpy as jnp
from jax import lax
from jax.experimental import pallas as pl
from jax.experimental.pallas import tpu as pltpu
from jax.sharding import PartitionSpec as P

ITERS = 2
GROUPS = 1
VMEM = 48 << 20
F32 = jnp.float32
BF16 = jnp.bfloat16
CONTRACT_FIRST = (((0,), (0,)), ((), ()))


def split_product(product, rank_mask, rank_most, right_count):
    real = product[..., :rank_most, :right_count] + product[..., rank_most:, right_count:]
    imaginary = product[..., :rank_most, right_count:] - product[..., rank_most:, :right_count]
    weights = rank_mask[..., None]
    return jnp.concatenate([real * weights, imaginary * weights], -1).astype(BF16)


def expand_complex(coefficient, right_count):
    real = coefficient[..., :right_count]
    imaginary = coefficient[..., right_count:]
    upper = jnp.concatenate([real, imaginary], -1)
    lower = jnp.concatenate([-imaginary, real], -1)
    return jnp.concatenate([upper, lower], -2)


def local_plain(u_factors, v_factors, ranks, model_init, observed, step):
    frequencies = model_init.shape[0]
    rank_most = u_factors.shape[-1] // 2
    right_count = model_init.shape[-1] // 2
    tile_size = u_factors.shape[2]
    rows_here = u_factors.shape[1]
    cols_here = u_factors.shape[3]
    rank_mask = (
        jnp.arange(rank_most, dtype=jnp.int32)[None, None, None, :] < ranks[..., None]
    ).astype(F32)
    model = model_init
    misfit = model_init
    for sweep in range(ITERS):
        gathered = lax.all_gather(model.astype(BF16), "row", axis=1, tiled=True)
        model_tiles = gathered.reshape(frequencies, cols_here, tile_size, 2 * right_count)
        product = jnp.einsum("fiajk,fjal->fijkl", v_factors, model_tiles, preferred_element_type=F32)
        coefficient = expand_complex(split_product(product, rank_mask, rank_most, right_count), right_count)
        partial_value = jnp.einsum("fiajk,fijkl->fial", u_factors, coefficient, preferred_element_type=F32)
        partial_value = partial_value.reshape(frequencies, rows_here * tile_size, 2 * right_count)
        predicted = lax.psum_scatter(partial_value, "col", scatter_dimension=1, tiled=True)
        misfit = predicted - observed
        misfit_half = lax.all_gather(misfit.astype(BF16), "col", axis=1, tiled=True)
        misfit_tiles = misfit_half.reshape(frequencies, rows_here, tile_size, 2 * right_count)
        product = jnp.einsum("fiajk,fial->fijkl", u_factors, misfit_tiles, preferred_element_type=F32)
        back = expand_complex(split_product(product, rank_mask, rank_most, right_count), right_count)
        gradient_part = jnp.einsum("fiajk,fijkl->fjal", v_factors, back, preferred_element_type=F32)
        gradient_part = gradient_part.reshape(frequencies, cols_here * tile_size, 2 * right_count)
        gradient = lax.psum_scatter(gradient_part, "row", scatter_dimension=1, tiled=True)
        model = model - step[:, None, None] * gradient
    return (model, misfit)


def tile_columns(ref, lead):
    tiles = jnp.swapaxes(ref[lead], 0, 1)
    return [tiles[j] for j in range(tiles.shape[0])]


def combine(product, rank):
    half_k = product.shape[0] // 2
    half_r = product.shape[1] // 2
    kept = lax.broadcasted_iota(jnp.int32, (half_k, half_r), 0) < rank
    zero = jnp.zeros((half_k, half_r), F32)
    real = product[:half_k, :half_r] + product[half_k:, half_r:]
    imaginary = product[:half_k, half_r:] - product[half_k:, :half_r]
    real = jnp.where(kept, real, zero).astype(BF16)
    imaginary = jnp.where(kept, imaginary, zero).astype(BF16)
    upper = jnp.concatenate([real, imaginary], 1)
    lower = jnp.concatenate([-imaginary, real], 1)
    return jnp.concatenate([upper, lower], 0)


def fetches(place, u_hbm, v_hbm, u_buf, v_buf, sems, items, shards, first, v_first):
    rows = u_buf.shape[1]
    u_copies, v_copies = [], []
    for n, (g, s) in enumerate(items):
        where = pl.ds(place[shards[s]] * rows, rows)
        u_copies.append(pltpu.make_async_copy(u_hbm.at[first + g, where], u_buf.at[n], sems.at[0, n]))
        v_copies.append(pltpu.make_async_copy(v_hbm.at[first + g, where], v_buf.at[n], sems.at[1, n]))
    if v_first:
        for v_copy, u_copy in zip(v_copies, u_copies):
            v_copy.start()
            u_copy.start()
    else:
        for copy in u_copies + v_copies:
            copy.start()
    return u_copies, v_copies


def forward_kernel(place, ranks, x_ref, u_hbm, v_hbm, *rest, first, items, shards):
    outs, (u_buf, v_buf, sems) = rest[:-3], rest[-3:]
    rows, size, cols, width = u_buf.shape[1:]
    members, block = x_ref.shape[1:3]
    u_copies, v_copies = fetches(place, u_hbm, v_hbm, u_buf, v_buf, sems, items, shards, first, True)
    for n, (g, s) in enumerate(items):
        v_copies[n].wait()
        right = [tile_columns(v_buf, (n, i)) for i in range(rows)]
        coefficient = [[] for i in range(rows)]
        for j in range(cols):
            member, inside = divmod(j * size, block)
            product = lax.dot_general(
                jnp.concatenate([right[i][j] for i in range(rows)], 1),
                x_ref[g, place[place.shape[0] - 1] ^ member, inside : inside + size, :],
                CONTRACT_FIRST,
                preferred_element_type=F32,
            )
            for i in range(rows):
                rank = ranks[first + g, place[shards[s]] * rows + i, j]
                coefficient[i].append(combine(product[i * width : (i + 1) * width], rank))
        u_copies[n].wait()
        for i in range(rows):
            outs[s][g, i * size : (i + 1) * size, :] = jnp.dot(
                jnp.concatenate(tile_columns(u_buf, (n, i)), 1),
                jnp.concatenate(coefficient[i], 0),
                preferred_element_type=F32,
            ).astype(outs[s].dtype)


def adjoint_kernel(place, ranks, u_hbm, v_hbm, *rest, first, items, shards, fresh):
    count = max(s for g, s in items) + 1
    r_refs, (out_ref, u_buf, v_buf, sems) = rest[:count], rest[-4:]
    rows, size, cols, width = u_buf.shape[1:]
    u_copies, v_copies = fetches(place, u_hbm, v_hbm, u_buf, v_buf, sems, items, shards, first, False)
    back = []
    for n, (g, s) in enumerate(items):
        u_copies[n].wait()
        for i in range(rows):
            product = lax.dot_general(
                jnp.concatenate(tile_columns(u_buf, (n, i)), 1),
                r_refs[s][g, i * size : (i + 1) * size, :],
                CONTRACT_FIRST,
                preferred_element_type=F32,
            )
            back.append(
                [
                    combine(
                        product[j * width : (j + 1) * width], ranks[first + g, place[shards[s]] * rows + i, j]
                    )
                    for j in range(cols)
                ]
            )
    for copy in v_copies:
        copy.wait()
    for g in range(out_ref.shape[0]):
        mine = [(n, i) for n, item in enumerate(items) if item[0] == g for i in range(rows)]
        right = [tile_columns(v_buf, at) for at in mine]
        for j in range(cols):
            added = jnp.dot(
                jnp.concatenate([tiles[j] for tiles in right], 1),
                jnp.concatenate([back[n * rows + i][j] for n, i in mine], 0),
                preferred_element_type=F32,
            )
            where = slice(j * size, (j + 1) * size)
            if fresh:
                out_ref[g, where, :] = added
            else:
                out_ref[g, where, :] += added


VMEM_SPEC = pl.BlockSpec(memory_space=pltpu.VMEM)
SMEM_SPEC = pl.BlockSpec(memory_space=pltpu.SMEM)
HBM_SPEC = pl.BlockSpec(memory_space=pltpu.HBM)


def buffers(count, rows, factors):
    shape = (count, rows) + factors.shape[2:]
    return [pltpu.VMEM(shape, BF16), pltpu.VMEM(shape, BF16), pltpu.SemaphoreType.DMA((2, count))]


def cost(count, rows, factors):
    size, cols, width = factors.shape[2:]
    flops = 8 * count * rows * size * cols * width * size
    return pl.CostEstimate(flops=flops, bytes_accessed=4 * count * rows * size * cols * width, transcendentals=0)


def forward(u, v, x, ranks, place, shards, first, rows, dtype):
    group, lines = x.shape[0], x.shape[3]
    many = len(shards)
    shards = tuple(k % (place.shape[0] - 1) for k in shards)
    items = [(g, s) for g in range(group) for s in range(many)]
    out = jax.ShapeDtypeStruct((group, rows * u.shape[2], lines), dtype)
    return pl.pallas_call(
        functools.partial(forward_kernel, first=first, items=items, shards=shards),
        out_shape=[out] * many,
        in_specs=[SMEM_SPEC, SMEM_SPEC, VMEM_SPEC, HBM_SPEC, HBM_SPEC],
        out_specs=[VMEM_SPEC] * many,
        scratch_shapes=buffers(len(items), rows, u),
        compiler_params=pltpu.CompilerParams(vmem_limit_bytes=VMEM),
        cost_estimate=cost(len(items), rows, u),
    )(place, ranks, x, u, v)


def adjoint(u, v, arrived, ranks, start, place, shards, first, rows):
    group, lines = arrived[0].shape[0], arrived[0].shape[2]
    many = len(arrived)
    shards = tuple(k % (place.shape[0] - 1) for k in shards)
    items = [(g, s) for g in range(group) for s in range(many)]
    more = [] if start is None else [start]
    return pl.pallas_call(
        functools.partial(adjoint_kernel, first=first, items=items, shards=shards, fresh=start is None),
        out_shape=jax.ShapeDtypeStruct((group, u.shape[3] * u.shape[2], lines), F32),
        in_specs=[SMEM_SPEC, SMEM_SPEC, HBM_SPEC, HBM_SPEC] + [VMEM_SPEC] * (many + len(more)),
        out_specs=VMEM_SPEC,
        input_output_aliases={4 + many: 0} if more else {},
        scratch_shapes=buffers(len(items), rows, u),
        compiler_params=pltpu.CompilerParams(vmem_limit_bytes=VMEM),
        cost_estimate=cost(len(items), rows, u),
    )(place, ranks, u, v, *arrived, *more)


def ring_order(count):
    return [2 * k for k in range(count // 2)] + [2 * k + 1 for k in reversed(range(count // 2))]


class Rings:
    def __init__(self, col_count):
        order = ring_order(col_count)
        self.fore = [(order[k], order[(k + 1) % col_count]) for k in range(col_count)]
        self.back = [(b, a) for a, b in self.fore]
        ahead_of = [[order[(order.index(c) + k) % col_count] for k in range(col_count)] for c in range(col_count)]
        mine = lax.dynamic_slice(jnp.array(ahead_of, jnp.int32), (lax.axis_index("col"), 0), (1, col_count))
        self.table = jnp.concatenate([mine[0], lax.axis_index("row").astype(jnp.int32)[None]])

    def ahead(self, x):
        return lax.ppermute(x, "col", self.fore)

    def behind(self, x):
        return lax.ppermute(x, "col", self.back)


def swap_core(x):
    return lax.ppermute(x, "row", [(k, k ^ 1) for k in range(4)])


def swap_chip(x):
    return lax.ppermute(x, "row", [(k, k ^ 2) for k in range(4)])


def gather_model(half):
    across = swap_chip(half)
    beside = swap_core(half)
    corner = swap_core(across)
    return jnp.stack([half, beside, across, corner], 1)


def scatter_gradient(total):
    group, count, lines = total.shape
    row = lax.axis_index("row")
    core = row & 1
    chip = row >> 1
    shards = total.reshape(group, 2, 2, count // 4, lines)

    def pick(x, c):
        return lax.dynamic_slice(shards, (0, x, c, 0, 0), (group, 1, 1, count // 4, lines)).reshape(
            group, count // 4, lines
        )

    far = pick(1 - chip, core) + swap_core(pick(1 - chip, 1 - core).astype(BF16)).astype(F32)
    other = swap_chip(far.astype(BF16))
    near = pick(chip, core) + swap_core(pick(chip, 1 - core).astype(BF16)).astype(F32)
    return near, other


def local_ring(u, v, ranks, model_init, observed, step, *, col_count):
    frequencies, tile_rows, size, cols, width = u.shape
    rows = tile_rows // col_count
    rings = Rings(col_count)
    far = col_count // 2
    cut = rows * size // 2
    group = frequencies // GROUPS
    models, misfits = [], []
    for first in range(0, frequencies, group):
        some = slice(first, first + group)
        model = model_init[some]
        for sweep in range(ITERS):
            x = gather_model(model.astype(BF16))
            (part,) = forward(u, v, x, ranks, rings.table, (far,), first, rows, BF16)
            fore = rings.ahead(part[:, :cut])
            back = rings.behind(part[:, cut:])
            for k in range(far - 1, 0, -1):
                up, down = forward(u, v, x, ranks, rings.table, (k, -k), first, rows, F32)
                if k == far - 1:
                    up = jnp.concatenate([up[:, :cut] + fore.astype(F32), up[:, cut:]], 1)
                    down = jnp.concatenate([down[:, :cut], down[:, cut:] + back.astype(F32)], 1)
                else:
                    up = up + fore.astype(F32)
                    down = down + back.astype(F32)
                fore = rings.ahead(up.astype(BF16))
                back = rings.behind(down.astype(BF16))
            (own,) = forward(u, v, x, ranks, rings.table, (0,), first, rows, F32)
            misfit = own + fore.astype(F32) + back.astype(F32) - observed[some]
            half = misfit.astype(BF16)
            fore = rings.ahead(half)
            back = rings.behind(half)
            total = adjoint(u, v, [half], ranks, None, rings.table, (0,), first, rows)
            for k in range(1, far):
                arrived = [fore, back]
                if k < far - 1:
                    fore, back = rings.ahead(fore), rings.behind(back)
                else:
                    fore, back = rings.ahead(fore[:, :cut]), rings.behind(back[:, cut:])
                total = adjoint(u, v, arrived, ranks, total, rings.table, (-k, k), first, rows)
            last = jnp.concatenate([fore, back], 1)
            total = adjoint(u, v, [last], ranks, total, rings.table, (far,), first, rows)
            near, other = scatter_gradient(total)
            model = model - step[some, None, None] * (near + other.astype(F32))
        models.append(model)
        misfits.append(misfit)
    return (jnp.concatenate(models, 0), jnp.concatenate(misfits, 0))


def solution(mesh):
    col_count, row_count = mesh.shape["col"], mesh.shape["row"]

    def local(u, v, ranks, model_init, observed, step):
        if row_count == 4 and col_count % 2 == 0 and col_count >= 4 and u.shape[1] % col_count == 0:
            return local_ring(u, v, ranks, model_init, observed, step, col_count=col_count)
        return local_plain(u, v, ranks, model_init, observed, step)

    return jax.shard_map(
        local,
        mesh=mesh,
        in_specs=(
            P(None, "row", None, "col", None),
            P(None, "row", None, "col", None),
            P(None, "row", "col"),
            P(None, ("col", "row"), None),
            P(None, ("row", "col"), None),
            P(),
        ),
        out_specs=(P(None, ("col", "row"), None), P(None, ("row", "col"), None)),
        check_vma=False,
    )
```

```python
import functools

import jax
import jax.numpy as jnp
from jax import lax
from jax.experimental import pallas as pl
from jax.experimental.pallas import tpu as pltpu
from jax.sharding import PartitionSpec as P

ITERS = 2
GROUPS = 2
VMEM = 11 << 20
SMALL_VMEM = 6 << 20
F32 = jnp.float32
BF16 = jnp.bfloat16
CONTRACT_FIRST = (((0,), (0,)), ((), ()))


def split_product(product, rank_mask, rank_most, right_count):
    real = product[..., :rank_most, :right_count] + product[..., rank_most:, right_count:]
    imaginary = product[..., :rank_most, right_count:] - product[..., rank_most:, :right_count]
    weights = rank_mask[..., None]
    return jnp.concatenate([real * weights, imaginary * weights], -1).astype(BF16)


def expand_complex(coefficient, right_count):
    real = coefficient[..., :right_count]
    imaginary = coefficient[..., right_count:]
    upper = jnp.concatenate([real, imaginary], -1)
    lower = jnp.concatenate([-imaginary, real], -1)
    return jnp.concatenate([upper, lower], -2)


def local_plain(u_factors, v_factors, ranks, model_init, observed, step):
    frequencies = model_init.shape[0]
    rank_most = u_factors.shape[-1] // 2
    right_count = model_init.shape[-1] // 2
    tile_size = u_factors.shape[2]
    rows_here = u_factors.shape[1]
    cols_here = u_factors.shape[3]
    rank_mask = (
        jnp.arange(rank_most, dtype=jnp.int32)[None, None, None, :] < ranks[..., None]
    ).astype(F32)
    model = model_init
    misfit = model_init
    for sweep in range(ITERS):
        gathered = lax.all_gather(model.astype(BF16), "row", axis=1, tiled=True)
        model_tiles = gathered.reshape(frequencies, cols_here, tile_size, 2 * right_count)
        product = jnp.einsum("fiajk,fjal->fijkl", v_factors, model_tiles, preferred_element_type=F32)
        coefficient = expand_complex(split_product(product, rank_mask, rank_most, right_count), right_count)
        partial_value = jnp.einsum("fiajk,fijkl->fial", u_factors, coefficient, preferred_element_type=F32)
        partial_value = partial_value.reshape(frequencies, rows_here * tile_size, 2 * right_count)
        predicted = lax.psum_scatter(partial_value, "col", scatter_dimension=1, tiled=True)
        misfit = predicted - observed
        misfit_half = lax.all_gather(misfit.astype(BF16), "col", axis=1, tiled=True)
        misfit_tiles = misfit_half.reshape(frequencies, rows_here, tile_size, 2 * right_count)
        product = jnp.einsum("fiajk,fial->fijkl", u_factors, misfit_tiles, preferred_element_type=F32)
        back = expand_complex(split_product(product, rank_mask, rank_most, right_count), right_count)
        gradient_part = jnp.einsum("fiajk,fijkl->fjal", v_factors, back, preferred_element_type=F32)
        gradient_part = gradient_part.reshape(frequencies, cols_here * tile_size, 2 * right_count)
        gradient = lax.psum_scatter(gradient_part, "row", scatter_dimension=1, tiled=True)
        model = model - step[:, None, None] * gradient
    return (model, misfit)


def tile_columns(ref, lead):
    tiles = jnp.swapaxes(ref[lead], 0, 1)
    return [tiles[j] for j in range(tiles.shape[0])]


def combine(product, rank):
    half_k = product.shape[0] // 2
    half_r = product.shape[1] // 2
    kept = lax.broadcasted_iota(jnp.int32, (half_k, half_r), 0) < rank
    zero = jnp.zeros((half_k, half_r), F32)
    real = product[:half_k, :half_r] + product[half_k:, half_r:]
    imaginary = product[:half_k, half_r:] - product[half_k:, :half_r]
    real = jnp.where(kept, real, zero).astype(BF16)
    imaginary = jnp.where(kept, imaginary, zero).astype(BF16)
    upper = jnp.concatenate([real, imaginary], 1)
    lower = jnp.concatenate([-imaginary, real], 1)
    return jnp.concatenate([upper, lower], 0)


def forward_kernel(place, ranks, x_ref, u_ref, v_ref, *outs, first, rows, items, shards):
    size, cols, width = u_ref.shape[2:]
    members, block = x_ref.shape[1:3]
    for g, s in items:
        row = place[shards[s]] * rows
        right = [tile_columns(v_ref, (first + g, row + i)) for i in range(rows)]
        coefficient = [[] for i in range(rows)]
        for j in range(cols):
            member, inside = divmod(j * size, block)
            product = lax.dot_general(
                jnp.concatenate([right[i][j] for i in range(rows)], 1),
                x_ref[g, place[place.shape[0] - 1] ^ member, inside : inside + size, :],
                CONTRACT_FIRST,
                preferred_element_type=F32,
            )
            for i in range(rows):
                rank = ranks[first + g, row + i, j]
                coefficient[i].append(combine(product[i * width : (i + 1) * width], rank))
        for i in range(rows):
            out, inside = divmod(i * size, outs[0].shape[1])
            out = outs[s * (len(outs) // len(shards)) + out]
            out[g, inside : inside + size, :] = jnp.dot(
                jnp.concatenate(tile_columns(u_ref, (first + g, row + i)), 1),
                jnp.concatenate(coefficient[i], 0),
                preferred_element_type=F32,
            ).astype(out.dtype)


def adjoint_kernel(place, ranks, u_ref, v_ref, *rest, first, rows, items, shards, fresh):
    count = len(rest) - (1 if fresh else 2)
    r_refs, out_ref = rest[:count], rest[-1]
    pieces = count // len(shards)
    size, cols, width = u_ref.shape[2:]
    back = []
    for g, s in items:
        row = place[shards[s]] * rows
        for i in range(rows):
            piece, inside = divmod(i * size, r_refs[0].shape[1])
            product = lax.dot_general(
                jnp.concatenate(tile_columns(u_ref, (first + g, row + i)), 1),
                r_refs[s * pieces + piece][g, inside : inside + size, :],
                CONTRACT_FIRST,
                preferred_element_type=F32,
            )
            back.append(
                [
                    combine(
                        product[j * width : (j + 1) * width], ranks[first + g, row + i, j]
                    )
                    for j in range(cols)
                ]
            )
    for g in range(out_ref.shape[0]):
        mine = [(n, i) for n, item in enumerate(items) if item[0] == g for i in range(rows)]
        right = [tile_columns(v_ref, (first + g, place[shards[items[n][1]]] * rows + i)) for n, i in mine]
        for j in range(cols):
            added = jnp.dot(
                jnp.concatenate([tiles[j] for tiles in right], 1),
                jnp.concatenate([back[n * rows + i][j] for n, i in mine], 0),
                preferred_element_type=F32,
            )
            where = slice(j * size, (j + 1) * size)
            if fresh:
                out_ref[g, where, :] = added
            else:
                out_ref[g, where, :] += added


VMEM_SPEC = pl.BlockSpec(memory_space=pltpu.VMEM)
HBM_SPEC = pl.BlockSpec(memory_space=pltpu.HBM)
SMEM_SPEC = pl.BlockSpec(memory_space=pltpu.SMEM)


def cost(count, rows, factors):
    size, cols, width = factors.shape[2:]
    flops = 8 * count * rows * size * cols * width * size
    return pl.CostEstimate(flops=flops, bytes_accessed=4 * count * rows * size * cols * width, transcendentals=0)


def forward(u, v, x, ranks, place, shards, first, rows, dtype, pieces=1):
    group, lines = x.shape[0], x.shape[3]
    many = len(shards)
    shards = tuple(k % (place.shape[0] - 1) for k in shards)
    items = [(g, s) for g in range(group) for s in range(many)]
    out = jax.ShapeDtypeStruct((group, rows * u.shape[2] // pieces, lines), dtype)
    return pl.pallas_call(
        functools.partial(forward_kernel, first=first, rows=rows, items=items, shards=shards),
        out_shape=[out] * (many * pieces),
        in_specs=[SMEM_SPEC, SMEM_SPEC, VMEM_SPEC, VMEM_SPEC, VMEM_SPEC],
        out_specs=[VMEM_SPEC] * (many * pieces),
        compiler_params=pltpu.CompilerParams(vmem_limit_bytes=VMEM),
        cost_estimate=cost(len(items), rows, u),
    )(place, ranks, x, u, v)


def adjoint(u, v, arrived, ranks, start, place, shards, first, rows):
    group, lines = arrived[0].shape[0], arrived[0].shape[2]
    many = len(arrived)
    shards = tuple(k % (place.shape[0] - 1) for k in shards)
    items = [(g, s) for g in range(group) for s in range(len(shards))]
    more = [] if start is None else [start]
    return pl.pallas_call(
        functools.partial(adjoint_kernel, first=first, rows=rows, items=items, shards=shards, fresh=start is None),
        out_shape=jax.ShapeDtypeStruct((group, u.shape[3] * u.shape[2], lines), F32),
        in_specs=[SMEM_SPEC, SMEM_SPEC, VMEM_SPEC, VMEM_SPEC] + [VMEM_SPEC] * (many + len(more)),
        out_specs=VMEM_SPEC,
        input_output_aliases={4 + many: 0} if more else {},
        compiler_params=pltpu.CompilerParams(vmem_limit_bytes=VMEM),
        cost_estimate=cost(len(items), rows, u),
    )(place, ranks, u, v, *arrived, *more)


def load_kernel(place, ranks, u_hbm, v_hbm, u_ref, v_ref, token_ref, sems):
    copies = [
        pltpu.make_async_copy(hbm.at[f], ref.at[f], sems.at[n, f])
        for n, (hbm, ref) in enumerate(((u_hbm, u_ref), (v_hbm, v_ref)))
        for f in range(u_ref.shape[0])
    ]
    for copy in copies:
        copy.start()
    token_ref[...] = jnp.zeros_like(token_ref)
    for copy in copies:
        copy.wait()


def load(u, v, place, ranks):
    return pl.pallas_call(
        load_kernel,
        out_shape=[
            jax.ShapeDtypeStruct(u.shape, u.dtype),
            jax.ShapeDtypeStruct(v.shape, v.dtype),
            jax.ShapeDtypeStruct((8, 128), F32),
        ],
        in_specs=[SMEM_SPEC, SMEM_SPEC, HBM_SPEC, HBM_SPEC],
        out_specs=[VMEM_SPEC, VMEM_SPEC, VMEM_SPEC],
        scratch_shapes=[pltpu.SemaphoreType.DMA((2, u.shape[0]))],
        compiler_params=pltpu.CompilerParams(vmem_limit_bytes=SMALL_VMEM),
        cost_estimate=pl.CostEstimate(flops=0, bytes_accessed=8 * u.size, transcendentals=0),
    )(place, ranks, u, v)


def small(kernel, outs, *args, scalars=0):
    return pl.pallas_call(
        kernel,
        out_shape=[jax.ShapeDtypeStruct(shape, dtype) for shape, dtype in outs],
        in_specs=[SMEM_SPEC] * scalars + [VMEM_SPEC] * (len(args) - scalars),
        out_specs=[VMEM_SPEC] * len(outs),
        compiler_params=pltpu.CompilerParams(vmem_limit_bytes=SMALL_VMEM),
    )(*args)


def small_result(kernel, whole, result, others, *args, scalars=0):
    group, shape, dtype = whole
    begun = [] if result is None else [result]
    return pl.pallas_call(
        kernel,
        out_shape=[jax.ShapeDtypeStruct(shape, dtype)] + [jax.ShapeDtypeStruct(*other) for other in others],
        in_specs=[SMEM_SPEC] * scalars + [VMEM_SPEC] * (len(args) - scalars) + [HBM_SPEC] * len(begun),
        out_specs=[HBM_SPEC] + [VMEM_SPEC] * len(others),
        scratch_shapes=[pltpu.VMEM((group,) + shape[1:], dtype), pltpu.SemaphoreType.DMA],
        input_output_aliases={len(args): 0} if begun else {},
        compiler_params=pltpu.CompilerParams(vmem_limit_bytes=SMALL_VMEM),
    )(*args, *begun)


def keep(part_ref, whole_ref, sem, first):
    copy = pltpu.make_async_copy(part_ref, whole_ref.at[pl.ds(first, part_ref.shape[0])], sem)
    copy.start()
    return copy


def stack_kernel(*refs):
    for member, ref in enumerate(refs[:-1]):
        refs[-1][:, member] = ref[...]


def misfit_of(own_ref, fore_ref, back_ref, observed_ref, first):
    observed = observed_ref[pl.ds(first, own_ref.shape[0])]
    return own_ref[...] + fore_ref[...].astype(F32) + back_ref[...].astype(F32) - observed


def misfit_kernel(own_ref, fore_ref, back_ref, observed_ref, half_ref, *, first):
    half_ref[...] = misfit_of(own_ref, fore_ref, back_ref, observed_ref, first).astype(BF16)


def misfit_last_kernel(own_ref, fore_ref, back_ref, observed_ref, *rest, first):
    out_ref, half_ref, part_ref, sem = rest[-4:]
    misfit = misfit_of(own_ref, fore_ref, back_ref, observed_ref, first)
    part_ref[...] = misfit
    copy = keep(part_ref, out_ref, sem, first)
    half_ref[...] = misfit.astype(BF16)
    copy.wait()


def after_kernel(token_ref, ref, out_ref):
    out_ref[...] = ref[...]


def add_kernel(own_ref, received_ref, sum_ref, *, at):
    if received_ref.shape[1] < own_ref.shape[1]:
        sum_ref[...] = own_ref[...].astype(BF16)
    rows = pl.ds(at, received_ref.shape[1])
    sum_ref[:, rows, :] = (own_ref[:, rows, :] + received_ref[...].astype(F32)).astype(BF16)


def add(own, received, at=0):
    return small(functools.partial(add_kernel, at=at), [(own.shape, BF16)], own, received)[0]


def part_of(place, total_ref, chip_flip, core_flip):
    member = place[place.shape[0] - 1] ^ (2 * chip_flip + core_flip)
    count = total_ref.shape[1] // 4
    return total_ref[:, pl.ds(member * count, count), :]


def outward_kernel(place, total_ref, far_ref, near_ref):
    far_ref[...] = part_of(place, total_ref, 1, 1).astype(BF16)
    near_ref[...] = part_of(place, total_ref, 0, 1).astype(BF16)


def across_kernel(place, total_ref, received_ref, out_ref):
    out_ref[...] = (part_of(place, total_ref, 1, 0) + received_ref[...].astype(F32)).astype(BF16)


def step_down(place, step, total_ref, near_ref, other_ref, model_ref, new_ref, first, model_first):
    total = part_of(place, total_ref, 0, 0) + near_ref[...].astype(F32) + other_ref[...].astype(F32)
    for g in range(total.shape[0]):
        new_ref[g] = model_ref[model_first + g] - step[first + g] * total[g]


def model_kernel(place, step, total_ref, near_ref, other_ref, model_ref, new_ref, half_ref, *, first, model_first):
    step_down(place, step, total_ref, near_ref, other_ref, model_ref, new_ref, first, model_first)
    half_ref[...] = new_ref[...].astype(BF16)


def model_last_kernel(place, step, total_ref, near_ref, other_ref, model_ref, *rest, first, model_first):
    out_ref, part_ref, sem = rest[-3:]
    step_down(place, step, total_ref, near_ref, other_ref, model_ref, part_ref, first, model_first)
    keep(part_ref, out_ref, sem, first).wait()


def ring_order(count):
    return [2 * k for k in range(count // 2)] + [2 * k + 1 for k in reversed(range(count // 2))]


class Rings:
    def __init__(self, col_count):
        order = ring_order(col_count)
        self.fore = [(order[k], order[(k + 1) % col_count]) for k in range(col_count)]
        self.back = [(b, a) for a, b in self.fore]
        ahead_of = [[order[(order.index(c) + k) % col_count] for k in range(col_count)] for c in range(col_count)]
        mine = lax.dynamic_slice(jnp.array(ahead_of, jnp.int32), (lax.axis_index("col"), 0), (1, col_count))
        self.table = jnp.concatenate([mine[0], lax.axis_index("row").astype(jnp.int32)[None]])

    def ahead(self, x):
        return lax.ppermute(x, "col", self.fore)

    def behind(self, x):
        return lax.ppermute(x, "col", self.back)


def swap_core(x):
    return lax.ppermute(x, "row", [(k, k ^ 1) for k in range(4)])


def swap_chip(x):
    return lax.ppermute(x, "row", [(k, k ^ 2) for k in range(4)])


def after(token, x):
    return small(after_kernel, [(x.shape, x.dtype)], token, x)[0]


def gather_model(half, token=None):
    across = swap_chip(half)
    beside = swap_core(half)
    if token is not None:
        across = after(token, across)
    corner = swap_core(across)
    group, count, lines = half.shape
    return small(stack_kernel, [((group, 4, count, lines), BF16)], half, beside, across, corner)[0]


def descend(total, model, model_first, step, place, first, result, last):
    group, lines = total.shape[0], total.shape[2]
    count = total.shape[1] // 4
    part = ((group, count, lines), BF16)
    far, near = small(outward_kernel, [part, part], place, total, scalars=1)
    (far,) = small(across_kernel, [part], place, total, swap_core(far), scalars=1)
    args = (place, step, total, swap_core(near), swap_chip(far), model)
    told = dict(first=first, model_first=model_first)
    if last:
        whole = (group, (step.shape[0], count, lines), F32)
        return small_result(functools.partial(model_last_kernel, **told), whole, result, [], *args, scalars=2)
    return small(functools.partial(model_kernel, **told), [((group, count, lines), F32), part], *args, scalars=2)


def local_ring(u, v, ranks, model_init, observed, step, *, col_count):
    frequencies, tile_rows, size, cols, width = u.shape
    rows = tile_rows // col_count
    rings = Rings(col_count)
    far = col_count // 2
    cut = rows * size // 2
    group = frequencies // GROUPS
    u, v, token = load(u, v, rings.table, ranks)
    model_out, misfit_out = None, None
    for first in range(0, frequencies, group):
        model, model_first = model_init, first
        half = model_init[first : first + group].astype(BF16)
        for sweep in range(ITERS):
            x = gather_model(half, None if sweep else token)
            fore, back = forward(u, v, x, ranks, rings.table, (far,), first, rows, BF16, 2)
            fore, back = rings.ahead(fore), rings.behind(back)
            for k in range(far - 1, 0, -1):
                up, down = forward(u, v, x, ranks, rings.table, (k, -k), first, rows, F32)
                fore = rings.ahead(add(up, fore))
                back = rings.behind(add(down, back, cut if k == far - 1 else 0))
            (own,) = forward(u, v, x, ranks, rings.table, (0,), first, rows, F32)
            args = (own, fore, back, observed)
            if sweep == ITERS - 1:
                kernel = functools.partial(misfit_last_kernel, first=first)
                misfit_out, half = small_result(
                    kernel, (group, observed.shape, F32), misfit_out, [(own.shape, BF16)], *args
                )
            else:
                (half,) = small(functools.partial(misfit_kernel, first=first), [(own.shape, BF16)], *args)
            fore = rings.ahead(half)
            back = rings.behind(half)
            total = adjoint(u, v, [half], ranks, None, rings.table, (0,), first, rows)
            for k in range(1, far):
                arrived = [fore, back]
                if k < far - 1:
                    fore, back = rings.ahead(fore), rings.behind(back)
                else:
                    fore, back = rings.ahead(fore[:, :cut]), rings.behind(back[:, cut:])
                total = adjoint(u, v, arrived, ranks, total, rings.table, (-k, k), first, rows)
            total = adjoint(u, v, [fore, back], ranks, total, rings.table, (far,), first, rows)
            if sweep == ITERS - 1:
                (model_out,) = descend(total, model, model_first, step, rings.table, first, model_out, True)
            else:
                model, half = descend(total, model, model_first, step, rings.table, first, None, False)
                model_first = 0
    return (model_out, misfit_out)


def solution(mesh):
    col_count, row_count = mesh.shape["col"], mesh.shape["row"]

    def local(u, v, ranks, model_init, observed, step):
        if row_count == 4 and col_count % 2 == 0 and col_count >= 4 and u.shape[1] % (2 * col_count) == 0:
            return local_ring(u, v, ranks, model_init, observed, step, col_count=col_count)
        return local_plain(u, v, ranks, model_init, observed, step)

    return jax.shard_map(
        local,
        mesh=mesh,
        in_specs=(
            P(None, "row", None, "col", None),
            P(None, "row", None, "col", None),
            P(None, "row", "col"),
            P(None, ("col", "row"), None),
            P(None, ("row", "col"), None),
            P(),
        ),
        out_specs=(P(None, ("col", "row"), None), P(None, ("row", "col"), None)),
        check_vma=False,
    )
```

```python
import functools

import jax
import jax.numpy as jnp
from jax import lax
from jax.experimental import pallas as pl
from jax.experimental.pallas import tpu as pltpu
from jax.sharding import PartitionSpec as P

ITERS = 2
GROUPS = 2
LAG = 4
VMEM = 11 << 20
SMALL_VMEM = 6 << 20
F32 = jnp.float32
BF16 = jnp.bfloat16
CONTRACT_FIRST = (((0,), (0,)), ((), ()))


def split_product(product, rank_mask, rank_most, right_count):
    real = product[..., :rank_most, :right_count] + product[..., rank_most:, right_count:]
    imaginary = product[..., :rank_most, right_count:] - product[..., rank_most:, :right_count]
    weights = rank_mask[..., None]
    return jnp.concatenate([real * weights, imaginary * weights], -1).astype(BF16)


def expand_complex(coefficient, right_count):
    real = coefficient[..., :right_count]
    imaginary = coefficient[..., right_count:]
    upper = jnp.concatenate([real, imaginary], -1)
    lower = jnp.concatenate([-imaginary, real], -1)
    return jnp.concatenate([upper, lower], -2)


def local_plain(u_factors, v_factors, ranks, model_init, observed, step):
    frequencies = model_init.shape[0]
    rank_most = u_factors.shape[-1] // 2
    right_count = model_init.shape[-1] // 2
    tile_size = u_factors.shape[2]
    rows_here = u_factors.shape[1]
    cols_here = u_factors.shape[3]
    rank_mask = (
        jnp.arange(rank_most, dtype=jnp.int32)[None, None, None, :] < ranks[..., None]
    ).astype(F32)
    model = model_init
    misfit = model_init
    for sweep in range(ITERS):
        gathered = lax.all_gather(model.astype(BF16), "row", axis=1, tiled=True)
        model_tiles = gathered.reshape(frequencies, cols_here, tile_size, 2 * right_count)
        product = jnp.einsum("fiajk,fjal->fijkl", v_factors, model_tiles, preferred_element_type=F32)
        coefficient = expand_complex(split_product(product, rank_mask, rank_most, right_count), right_count)
        partial_value = jnp.einsum("fiajk,fijkl->fial", u_factors, coefficient, preferred_element_type=F32)
        partial_value = partial_value.reshape(frequencies, rows_here * tile_size, 2 * right_count)
        predicted = lax.psum_scatter(partial_value, "col", scatter_dimension=1, tiled=True)
        misfit = predicted - observed
        misfit_half = lax.all_gather(misfit.astype(BF16), "col", axis=1, tiled=True)
        misfit_tiles = misfit_half.reshape(frequencies, rows_here, tile_size, 2 * right_count)
        product = jnp.einsum("fiajk,fial->fijkl", u_factors, misfit_tiles, preferred_element_type=F32)
        back = expand_complex(split_product(product, rank_mask, rank_most, right_count), right_count)
        gradient_part = jnp.einsum("fiajk,fijkl->fjal", v_factors, back, preferred_element_type=F32)
        gradient_part = gradient_part.reshape(frequencies, cols_here * tile_size, 2 * right_count)
        gradient = lax.psum_scatter(gradient_part, "row", scatter_dimension=1, tiled=True)
        model = model - step[:, None, None] * gradient
    return (model, misfit)


def tile_columns(ref, lead):
    tiles = jnp.swapaxes(ref[lead], 0, 1)
    return [tiles[j] for j in range(tiles.shape[0])]


def combine(product, rank):
    half_k = product.shape[0] // 2
    half_r = product.shape[1] // 2
    kept = lax.broadcasted_iota(jnp.int32, (half_k, half_r), 0) < rank
    zero = jnp.zeros((half_k, half_r), F32)
    real = product[:half_k, :half_r] + product[half_k:, half_r:]
    imaginary = product[:half_k, half_r:] - product[half_k:, :half_r]
    real = jnp.where(kept, real, zero).astype(BF16)
    imaginary = jnp.where(kept, imaginary, zero).astype(BF16)
    upper = jnp.concatenate([real, imaginary], 1)
    lower = jnp.concatenate([-imaginary, real], 1)
    return jnp.concatenate([upper, lower], 0)


def forward_kernel(place, ranks, x_ref, u_ref, v_ref, *outs, first, rows, items, shards):
    size, cols, width = u_ref.shape[2:]
    members, block = x_ref.shape[1:3]
    for g, s in items:
        row = place[shards[s]] * rows
        right = [tile_columns(v_ref, (first + g, row + i)) for i in range(rows)]
        coefficient = [[] for i in range(rows)]
        for j in range(cols):
            member, inside = divmod(j * size, block)
            product = lax.dot_general(
                jnp.concatenate([right[i][j] for i in range(rows)], 1),
                x_ref[g, place[place.shape[0] - 1] ^ member, inside : inside + size, :],
                CONTRACT_FIRST,
                preferred_element_type=F32,
            )
            for i in range(rows):
                rank = ranks[first + g, row + i, j]
                coefficient[i].append(combine(product[i * width : (i + 1) * width], rank))
        for i in range(rows):
            out, inside = divmod(i * size, outs[0].shape[1])
            out = outs[s * (len(outs) // len(shards)) + out]
            out[g, inside : inside + size, :] = jnp.dot(
                jnp.concatenate(tile_columns(u_ref, (first + g, row + i)), 1),
                jnp.concatenate(coefficient[i], 0),
                preferred_element_type=F32,
            ).astype(out.dtype)


def adjoint_kernel(place, ranks, u_ref, v_ref, *rest, first, rows, items, shards, fresh):
    count = len(rest) - (1 if fresh else 2)
    r_refs, out_ref = rest[:count], rest[-1]
    pieces = count // len(shards)
    size, cols, width = u_ref.shape[2:]
    back = []
    for g, s in items:
        row = place[shards[s]] * rows
        for i in range(rows):
            piece, inside = divmod(i * size, r_refs[0].shape[1])
            product = lax.dot_general(
                jnp.concatenate(tile_columns(u_ref, (first + g, row + i)), 1),
                r_refs[s * pieces + piece][g, inside : inside + size, :],
                CONTRACT_FIRST,
                preferred_element_type=F32,
            )
            back.append(
                [
                    combine(
                        product[j * width : (j + 1) * width], ranks[first + g, row + i, j]
                    )
                    for j in range(cols)
                ]
            )
    for g in range(out_ref.shape[0]):
        mine = [(n, i) for n, item in enumerate(items) if item[0] == g for i in range(rows)]
        right = [tile_columns(v_ref, (first + g, place[shards[items[n][1]]] * rows + i)) for n, i in mine]
        for j in range(cols):
            added = jnp.dot(
                jnp.concatenate([tiles[j] for tiles in right], 1),
                jnp.concatenate([back[n * rows + i][j] for n, i in mine], 0),
                preferred_element_type=F32,
            )
            where = slice(j * size, (j + 1) * size)
            if fresh:
                out_ref[g, where, :] = added
            else:
                out_ref[g, where, :] += added


VMEM_SPEC = pl.BlockSpec(memory_space=pltpu.VMEM)
HBM_SPEC = pl.BlockSpec(memory_space=pltpu.HBM)
SMEM_SPEC = pl.BlockSpec(memory_space=pltpu.SMEM)


def cost(count, rows, factors):
    size, cols, width = factors.shape[2:]
    flops = 8 * count * rows * size * cols * width * size
    return pl.CostEstimate(flops=flops, bytes_accessed=4 * count * rows * size * cols * width, transcendentals=0)


class Order:
    def __init__(self, token):
        self.token = token

    def call(self, kernel, outs, args, in_specs, out_specs, scratch=(), aliases=None, limit=None, estimate=None):
        n_in, n_out = len(args), len(outs)

        def run(*refs):
            refs[n_in + 1 + n_out][...] = jnp.zeros((8, 128), F32)
            kernel(*refs[:n_in], *refs[n_in + 1 : n_in + 1 + n_out], *refs[n_in + 2 + n_out :])

        *results, self.token = pl.pallas_call(
            run,
            out_shape=[*outs, jax.ShapeDtypeStruct((8, 128), F32)],
            in_specs=[*in_specs, VMEM_SPEC],
            out_specs=[*out_specs, VMEM_SPEC],
            scratch_shapes=list(scratch),
            input_output_aliases=aliases or {},
            compiler_params=pltpu.CompilerParams(vmem_limit_bytes=limit or SMALL_VMEM),
            cost_estimate=estimate,
        )(*args, self.token)
        return results


def forward(order, u, v, x, ranks, place, shards, first, rows, dtype, pieces=1):
    group, lines = x.shape[0], x.shape[3]
    many = len(shards)
    shards = tuple(k % (place.shape[0] - 1) for k in shards)
    items = [(g, s) for g in range(group) for s in range(many)]
    out = jax.ShapeDtypeStruct((group, rows * u.shape[2] // pieces, lines), dtype)
    return order.call(
        functools.partial(forward_kernel, first=first, rows=rows, items=items, shards=shards),
        [out] * (many * pieces),
        (place, ranks, x, u, v),
        [SMEM_SPEC, SMEM_SPEC, VMEM_SPEC, VMEM_SPEC, VMEM_SPEC],
        [VMEM_SPEC] * (many * pieces),
        limit=VMEM,
        estimate=cost(len(items), rows, u),
    )


def adjoint(order, u, v, arrived, ranks, start, place, shards, first, rows):
    group, lines = arrived[0].shape[0], arrived[0].shape[2]
    many = len(arrived)
    shards = tuple(k % (place.shape[0] - 1) for k in shards)
    items = [(g, s) for g in range(group) for s in range(len(shards))]
    more = [] if start is None else [start]
    return order.call(
        functools.partial(adjoint_kernel, first=first, rows=rows, items=items, shards=shards, fresh=start is None),
        [jax.ShapeDtypeStruct((group, u.shape[3] * u.shape[2], lines), F32)],
        (place, ranks, u, v, *arrived, *more),
        [SMEM_SPEC, SMEM_SPEC] + [VMEM_SPEC] * (2 + many + len(more)),
        [VMEM_SPEC],
        aliases={4 + many: 0} if more else None,
        limit=VMEM,
        estimate=cost(len(items), rows, u),
    )[0]


def load_kernel(place, ranks, u_hbm, v_hbm, u_ref, v_ref, token_ref, sems):
    copies = [
        pltpu.make_async_copy(hbm.at[f], ref.at[f], sems.at[n, f])
        for n, (hbm, ref) in enumerate(((u_hbm, u_ref), (v_hbm, v_ref)))
        for f in range(u_ref.shape[0])
    ]
    for copy in copies:
        copy.start()
    token_ref[...] = jnp.zeros_like(token_ref)
    for copy in copies:
        copy.wait()


def load(u, v, place, ranks):
    return pl.pallas_call(
        load_kernel,
        out_shape=[
            jax.ShapeDtypeStruct(u.shape, u.dtype),
            jax.ShapeDtypeStruct(v.shape, v.dtype),
            jax.ShapeDtypeStruct((8, 128), F32),
        ],
        in_specs=[SMEM_SPEC, SMEM_SPEC, HBM_SPEC, HBM_SPEC],
        out_specs=[VMEM_SPEC, VMEM_SPEC, VMEM_SPEC],
        scratch_shapes=[pltpu.SemaphoreType.DMA((2, u.shape[0]))],
        compiler_params=pltpu.CompilerParams(vmem_limit_bytes=SMALL_VMEM),
        cost_estimate=pl.CostEstimate(flops=0, bytes_accessed=8 * u.size, transcendentals=0),
    )(place, ranks, u, v)


def small(kernel, outs, *args, scalars=0, order=None):
    in_specs = [SMEM_SPEC] * scalars + [VMEM_SPEC] * (len(args) - scalars)
    out_specs = [VMEM_SPEC] * len(outs)
    outs = [jax.ShapeDtypeStruct(shape, dtype) for shape, dtype in outs]
    if order is not None:
        return order.call(kernel, outs, args, in_specs, out_specs)
    return pl.pallas_call(
        kernel,
        out_shape=outs,
        in_specs=in_specs,
        out_specs=out_specs,
        compiler_params=pltpu.CompilerParams(vmem_limit_bytes=SMALL_VMEM),
    )(*args)


def small_result(order, kernel, whole, result, others, *args, scalars=0):
    group, shape, dtype = whole
    begun = [] if result is None else [result]
    return order.call(
        kernel,
        [jax.ShapeDtypeStruct(shape, dtype)] + [jax.ShapeDtypeStruct(*other) for other in others],
        (*args, *begun),
        [SMEM_SPEC] * scalars + [VMEM_SPEC] * (len(args) - scalars) + [HBM_SPEC] * len(begun),
        [HBM_SPEC] + [VMEM_SPEC] * len(others),
        scratch=[pltpu.VMEM((group,) + shape[1:], dtype), pltpu.SemaphoreType.DMA],
        aliases={len(args): 0} if begun else None,
    )


def keep(part_ref, whole_ref, sem, first):
    copy = pltpu.make_async_copy(part_ref, whole_ref.at[pl.ds(first, part_ref.shape[0])], sem)
    copy.start()
    return copy


def stack_kernel(*refs):
    for member, ref in enumerate(refs[:-1]):
        refs[-1][:, member] = ref[...]


def misfit_of(own_ref, fore_ref, back_ref, observed_ref, first):
    observed = observed_ref[pl.ds(first, own_ref.shape[0])]
    return own_ref[...] + fore_ref[...].astype(F32) + back_ref[...].astype(F32) - observed


def misfit_kernel(own_ref, fore_ref, back_ref, observed_ref, half_ref, *, first):
    half_ref[...] = misfit_of(own_ref, fore_ref, back_ref, observed_ref, first).astype(BF16)


def misfit_last_kernel(own_ref, fore_ref, back_ref, observed_ref, *rest, first):
    out_ref, half_ref, part_ref, sem = rest[-4:]
    misfit = misfit_of(own_ref, fore_ref, back_ref, observed_ref, first)
    part_ref[...] = misfit
    copy = keep(part_ref, out_ref, sem, first)
    half_ref[...] = misfit.astype(BF16)
    copy.wait()


def after_kernel(token_ref, ref, out_ref):
    out_ref[...] = ref[...]


def add_kernel(own_ref, received_ref, sum_ref, *, at):
    if received_ref.shape[1] < own_ref.shape[1]:
        sum_ref[...] = own_ref[...].astype(BF16)
    rows = pl.ds(at, received_ref.shape[1])
    sum_ref[:, rows, :] = (own_ref[:, rows, :] + received_ref[...].astype(F32)).astype(BF16)


def add(own, received, at=0):
    return small(functools.partial(add_kernel, at=at), [(own.shape, BF16)], own, received)[0]


def part_of(place, total_ref, chip_flip, core_flip):
    member = place[place.shape[0] - 1] ^ (2 * chip_flip + core_flip)
    count = total_ref.shape[1] // 4
    return total_ref[:, pl.ds(member * count, count), :]


def outward_kernel(place, total_ref, far_ref, near_ref):
    far_ref[...] = part_of(place, total_ref, 1, 1).astype(BF16)
    near_ref[...] = part_of(place, total_ref, 0, 1).astype(BF16)


def across_kernel(place, total_ref, received_ref, out_ref):
    out_ref[...] = (part_of(place, total_ref, 1, 0) + received_ref[...].astype(F32)).astype(BF16)


def step_down(place, step, total_ref, near_ref, other_ref, model_ref, new_ref, first, model_first):
    total = part_of(place, total_ref, 0, 0) + near_ref[...].astype(F32) + other_ref[...].astype(F32)
    for g in range(total.shape[0]):
        new_ref[g] = model_ref[model_first + g] - step[first + g] * total[g]


def model_kernel(place, step, total_ref, near_ref, other_ref, model_ref, new_ref, half_ref, *, first, model_first):
    step_down(place, step, total_ref, near_ref, other_ref, model_ref, new_ref, first, model_first)
    half_ref[...] = new_ref[...].astype(BF16)


def model_last_kernel(place, step, total_ref, near_ref, other_ref, model_ref, *rest, first, model_first):
    out_ref, part_ref, sem = rest[-3:]
    step_down(place, step, total_ref, near_ref, other_ref, model_ref, part_ref, first, model_first)
    keep(part_ref, out_ref, sem, first).wait()


def ring_order(count):
    return [2 * k for k in range(count // 2)] + [2 * k + 1 for k in reversed(range(count // 2))]


class Rings:
    def __init__(self, col_count):
        self.count = col_count
        order = ring_order(col_count)
        self.fore = [(order[k], order[(k + 1) % col_count]) for k in range(col_count)]
        self.back = [(b, a) for a, b in self.fore]
        ahead_of = [[order[(order.index(c) + k) % col_count] for k in range(col_count)] for c in range(col_count)]
        mine = lax.dynamic_slice(jnp.array(ahead_of, jnp.int32), (lax.axis_index("col"), 0), (1, col_count))
        self.table = jnp.concatenate([mine[0], lax.axis_index("row").astype(jnp.int32)[None]])

    def ahead(self, x):
        return lax.ppermute(x, "col", self.fore)

    def behind(self, x):
        return lax.ppermute(x, "col", self.back)


def swap_core(x):
    return lax.ppermute(x, "row", [(k, k ^ 1) for k in range(4)])


def swap_chip(x):
    return lax.ppermute(x, "row", [(k, k ^ 2) for k in range(4)])


def after(token, x):
    return small(after_kernel, [(x.shape, x.dtype)], token, x)[0]


def gather_model(half, token=None):
    across = swap_chip(half)
    beside = swap_core(half)
    if token is not None:
        across = after(token, across)
    corner = swap_core(across)
    group, count, lines = half.shape
    return small(stack_kernel, [((group, 4, count, lines), BF16)], half, beside, across, corner)[0]


class Results:
    model = None
    misfit = None


def flow(order, rings, results, u, v, ranks, model_init, observed, step, first, group, token):
    size = u.shape[2]
    rows = u.shape[1] // rings.count
    far = rings.count // 2
    cut = rows * size // 2
    place = rings.table
    model, model_first = model_init, first
    half = model_init[first : first + group].astype(BF16)
    for sweep in range(ITERS):
        final = sweep == ITERS - 1
        x = gather_model(half, None if sweep else token)
        fore, back = forward(order, u, v, x, ranks, place, (far,), first, rows, BF16, 2)
        fore, back = rings.ahead(fore), rings.behind(back)
        yield
        for k in range(far - 1, 0, -1):
            up, down = forward(order, u, v, x, ranks, place, (k, -k), first, rows, F32)
            fore = rings.ahead(add(up, fore))
            back = rings.behind(add(down, back, cut if k == far - 1 else 0))
            yield
        (own,) = forward(order, u, v, x, ranks, place, (0,), first, rows, F32)
        args = (own, fore, back, observed)
        if final:
            kernel = functools.partial(misfit_last_kernel, first=first)
            whole = (group, observed.shape, F32)
            results.misfit, half = small_result(order, kernel, whole, results.misfit, [(own.shape, BF16)], *args)
        else:
            (half,) = small(functools.partial(misfit_kernel, first=first), [(own.shape, BF16)], *args, order=order)
        fore, back = rings.ahead(half), rings.behind(half)
        yield
        total = adjoint(order, u, v, [half], ranks, None, place, (0,), first, rows)
        yield
        for k in range(1, far):
            arrived = [fore, back]
            if k < far - 1:
                fore, back = rings.ahead(fore), rings.behind(back)
            else:
                fore, back = rings.ahead(fore[:, :cut]), rings.behind(back[:, cut:])
            total = adjoint(order, u, v, arrived, ranks, total, place, (-k, k), first, rows)
            yield
        total = adjoint(order, u, v, [fore, back], ranks, total, place, (far,), first, rows)
        lines = total.shape[2]
        count = total.shape[1] // 4
        part = ((group, count, lines), BF16)
        out, near = small(outward_kernel, [part, part], place, total, scalars=1, order=order)
        out, near = swap_core(out), swap_core(near)
        yield
        (out,) = small(across_kernel, [part], place, total, out, scalars=1, order=order)
        out = swap_chip(out)
        yield
        args = (place, step, total, near, out, model)
        told = dict(first=first, model_first=model_first)
        if final:
            whole = (group, (step.shape[0], count, lines), F32)
            kernel = functools.partial(model_last_kernel, **told)
            (results.model,) = small_result(order, kernel, whole, results.model, [], *args, scalars=2)
        else:
            outs = [((group, count, lines), F32), part]
            kernel = functools.partial(model_kernel, **told)
            model, half = small(kernel, outs, *args, scalars=2, order=order)
            model_first = 0
        yield


def local_ring(u, v, ranks, model_init, observed, step, *, col_count):
    frequencies = u.shape[0]
    rings = Rings(col_count)
    u, v, token = load(u, v, rings.table, ranks)
    order, results = Order(token), Results()
    group = frequencies // GROUPS
    firsts = range(0, frequencies, group)
    flows = [
        flow(order, rings, results, u, v, ranks, model_init, observed, step, first, group, token) for first in firsts
    ]
    waits = [LAG * n for n in range(GROUPS)]
    running = [True] * GROUPS
    while any(running):
        for n, work in enumerate(flows):
            if waits[n] > 0:
                waits[n] -= 1
            elif running[n]:
                running[n] = next(work, work) is not work
    return (results.model, results.misfit)


def solution(mesh):
    col_count, row_count = mesh.shape["col"], mesh.shape["row"]

    def local(u, v, ranks, model_init, observed, step):
        if row_count == 4 and col_count % 2 == 0 and col_count >= 4 and u.shape[1] % (2 * col_count) == 0:
            return local_ring(u, v, ranks, model_init, observed, step, col_count=col_count)
        return local_plain(u, v, ranks, model_init, observed, step)

    return jax.shard_map(
        local,
        mesh=mesh,
        in_specs=(
            P(None, "row", None, "col", None),
            P(None, "row", None, "col", None),
            P(None, "row", "col"),
            P(None, ("col", "row"), None),
            P(None, ("row", "col"), None),
            P(),
        ),
        out_specs=(P(None, ("col", "row"), None), P(None, ("row", "col"), None)),
        check_vma=False,
    )
```

```python
import functools

import jax
import jax.numpy as jnp
from jax import lax
from jax.experimental import pallas as pl
from jax.experimental.pallas import tpu as pltpu
from jax.sharding import PartitionSpec as P

ITERS = 2
GROUPS = 2
LAG = 4
VMEM = 11 << 20
SMALL_VMEM = 6 << 20
F32 = jnp.float32
BF16 = jnp.bfloat16
CONTRACT_FIRST = (((0,), (0,)), ((), ()))


def split_product(product, rank_mask, rank_most, right_count):
    real = product[..., :rank_most, :right_count] + product[..., rank_most:, right_count:]
    imaginary = product[..., :rank_most, right_count:] - product[..., rank_most:, :right_count]
    weights = rank_mask[..., None]
    return jnp.concatenate([real * weights, imaginary * weights], -1).astype(BF16)


def expand_complex(coefficient, right_count):
    real = coefficient[..., :right_count]
    imaginary = coefficient[..., right_count:]
    upper = jnp.concatenate([real, imaginary], -1)
    lower = jnp.concatenate([-imaginary, real], -1)
    return jnp.concatenate([upper, lower], -2)


def local_plain(u_factors, v_factors, ranks, model_init, observed, step):
    frequencies = model_init.shape[0]
    rank_most = u_factors.shape[-1] // 2
    right_count = model_init.shape[-1] // 2
    tile_size = u_factors.shape[2]
    rows_here = u_factors.shape[1]
    cols_here = u_factors.shape[3]
    rank_mask = (
        jnp.arange(rank_most, dtype=jnp.int32)[None, None, None, :] < ranks[..., None]
    ).astype(F32)
    model = model_init
    misfit = model_init
    for sweep in range(ITERS):
        gathered = lax.all_gather(model.astype(BF16), "row", axis=1, tiled=True)
        model_tiles = gathered.reshape(frequencies, cols_here, tile_size, 2 * right_count)
        product = jnp.einsum("fiajk,fjal->fijkl", v_factors, model_tiles, preferred_element_type=F32)
        coefficient = expand_complex(split_product(product, rank_mask, rank_most, right_count), right_count)
        partial_value = jnp.einsum("fiajk,fijkl->fial", u_factors, coefficient, preferred_element_type=F32)
        partial_value = partial_value.reshape(frequencies, rows_here * tile_size, 2 * right_count)
        predicted = lax.psum_scatter(partial_value, "col", scatter_dimension=1, tiled=True)
        misfit = predicted - observed
        misfit_half = lax.all_gather(misfit.astype(BF16), "col", axis=1, tiled=True)
        misfit_tiles = misfit_half.reshape(frequencies, rows_here, tile_size, 2 * right_count)
        product = jnp.einsum("fiajk,fial->fijkl", u_factors, misfit_tiles, preferred_element_type=F32)
        back = expand_complex(split_product(product, rank_mask, rank_most, right_count), right_count)
        gradient_part = jnp.einsum("fiajk,fijkl->fjal", v_factors, back, preferred_element_type=F32)
        gradient_part = gradient_part.reshape(frequencies, cols_here * tile_size, 2 * right_count)
        gradient = lax.psum_scatter(gradient_part, "row", scatter_dimension=1, tiled=True)
        model = model - step[:, None, None] * gradient
    return (model, misfit)


def tile_columns(ref, lead):
    tiles = jnp.swapaxes(ref[lead], 0, 1)
    return [tiles[j] for j in range(tiles.shape[0])]


def combine(product, rank):
    half_k = product.shape[0] // 2
    half_r = product.shape[1] // 2
    kept = lax.broadcasted_iota(jnp.int32, (half_k, half_r), 0) < rank
    zero = jnp.zeros((half_k, half_r), F32)
    real = product[:half_k, :half_r] + product[half_k:, half_r:]
    imaginary = product[:half_k, half_r:] - product[half_k:, :half_r]
    real = jnp.where(kept, real, zero).astype(BF16)
    imaginary = jnp.where(kept, imaginary, zero).astype(BF16)
    upper = jnp.concatenate([real, imaginary], 1)
    lower = jnp.concatenate([-imaginary, real], 1)
    return jnp.concatenate([upper, lower], 0)


def forward_kernel(place, ranks, x_ref, u_ref, v_ref, *outs, first, rows, items, shards):
    size, cols, width = u_ref.shape[2:]
    members, block = x_ref.shape[1:3]
    for g, s in items:
        row = place[shards[s]] * rows
        right = [tile_columns(v_ref, (g, row + i)) for i in range(rows)]
        coefficient = [[] for i in range(rows)]
        for j in range(cols):
            member, inside = divmod(j * size, block)
            product = lax.dot_general(
                jnp.concatenate([right[i][j] for i in range(rows)], 1),
                x_ref[g, place[place.shape[0] - 1] ^ member, inside : inside + size, :],
                CONTRACT_FIRST,
                preferred_element_type=F32,
            )
            for i in range(rows):
                rank = ranks[first + g, row + i, j]
                coefficient[i].append(combine(product[i * width : (i + 1) * width], rank))
        for i in range(rows):
            out, inside = divmod(i * size, outs[0].shape[1])
            out = outs[s * (len(outs) // len(shards)) + out]
            out[g, inside : inside + size, :] = jnp.dot(
                jnp.concatenate(tile_columns(u_ref, (g, row + i)), 1),
                jnp.concatenate(coefficient[i], 0),
                preferred_element_type=F32,
            ).astype(out.dtype)


def adjoint_kernel(place, ranks, u_ref, v_ref, *rest, first, rows, items, shards, fresh):
    count = len(rest) - (1 if fresh else 2)
    r_refs, out_ref = rest[:count], rest[-1]
    pieces = count // len(shards)
    size, cols, width = u_ref.shape[2:]
    back = []
    for g, s in items:
        row = place[shards[s]] * rows
        for i in range(rows):
            piece, inside = divmod(i * size, r_refs[0].shape[1])
            product = lax.dot_general(
                jnp.concatenate(tile_columns(u_ref, (g, row + i)), 1),
                r_refs[s * pieces + piece][g, inside : inside + size, :],
                CONTRACT_FIRST,
                preferred_element_type=F32,
            )
            back.append(
                [
                    combine(
                        product[j * width : (j + 1) * width], ranks[first + g, row + i, j]
                    )
                    for j in range(cols)
                ]
            )
    for g in range(out_ref.shape[0]):
        mine = [(n, i) for n, item in enumerate(items) if item[0] == g for i in range(rows)]
        right = [tile_columns(v_ref, (g, place[shards[items[n][1]]] * rows + i)) for n, i in mine]
        for j in range(cols):
            added = jnp.dot(
                jnp.concatenate([tiles[j] for tiles in right], 1),
                jnp.concatenate([back[n * rows + i][j] for n, i in mine], 0),
                preferred_element_type=F32,
            )
            where = slice(j * size, (j + 1) * size)
            if fresh:
                out_ref[g, where, :] = added
            else:
                out_ref[g, where, :] += added


VMEM_SPEC = pl.BlockSpec(memory_space=pltpu.VMEM)
HBM_SPEC = pl.BlockSpec(memory_space=pltpu.HBM)
SMEM_SPEC = pl.BlockSpec(memory_space=pltpu.SMEM)


def cost(count, rows, factors):
    size, cols, width = factors.shape[2:]
    flops = 8 * count * rows * size * cols * width * size
    return pl.CostEstimate(flops=flops, bytes_accessed=4 * count * rows * size * cols * width, transcendentals=0)


class Order:
    def __init__(self, token):
        self.token = token

    def call(self, kernel, outs, args, in_specs, out_specs, scratch=(), aliases=None, limit=None, estimate=None):
        n_in, n_out = len(args), len(outs)

        def run(*refs):
            refs[n_in + 1 + n_out][...] = jnp.zeros((8, 128), F32)
            kernel(*refs[:n_in], *refs[n_in + 1 : n_in + 1 + n_out], *refs[n_in + 2 + n_out :])

        *results, self.token = pl.pallas_call(
            run,
            out_shape=[*outs, jax.ShapeDtypeStruct((8, 128), F32)],
            in_specs=[*in_specs, VMEM_SPEC],
            out_specs=[*out_specs, VMEM_SPEC],
            scratch_shapes=list(scratch),
            input_output_aliases=aliases or {},
            compiler_params=pltpu.CompilerParams(vmem_limit_bytes=limit or SMALL_VMEM),
            cost_estimate=estimate,
        )(*args, self.token)
        return results


def forward(order, u, v, x, ranks, place, shards, first, rows, dtype, pieces=1):
    group, lines = x.shape[0], x.shape[3]
    many = len(shards)
    shards = tuple(k % (place.shape[0] - 1) for k in shards)
    items = [(g, s) for g in range(group) for s in range(many)]
    out = jax.ShapeDtypeStruct((group, rows * u.shape[2] // pieces, lines), dtype)
    return order.call(
        functools.partial(forward_kernel, first=first, rows=rows, items=items, shards=shards),
        [out] * (many * pieces),
        (place, ranks, x, u, v),
        [SMEM_SPEC, SMEM_SPEC, VMEM_SPEC, VMEM_SPEC, VMEM_SPEC],
        [VMEM_SPEC] * (many * pieces),
        limit=VMEM,
        estimate=cost(len(items), rows, u),
    )


def adjoint(order, u, v, arrived, ranks, start, place, shards, first, rows):
    group, lines = arrived[0].shape[0], arrived[0].shape[2]
    many = len(arrived)
    shards = tuple(k % (place.shape[0] - 1) for k in shards)
    items = [(g, s) for g in range(group) for s in range(len(shards))]
    more = [] if start is None else [start]
    return order.call(
        functools.partial(adjoint_kernel, first=first, rows=rows, items=items, shards=shards, fresh=start is None),
        [jax.ShapeDtypeStruct((group, u.shape[3] * u.shape[2], lines), F32)],
        (place, ranks, u, v, *arrived, *more),
        [SMEM_SPEC, SMEM_SPEC] + [VMEM_SPEC] * (2 + many + len(more)),
        [VMEM_SPEC],
        aliases={4 + many: 0} if more else None,
        limit=VMEM,
        estimate=cost(len(items), rows, u),
    )[0]


def load_kernel(place, ranks, *refs, first):
    count = (len(refs) - 1) // 2
    sems = refs[-1]
    copies = [
        pltpu.make_async_copy(hbm.at[first + g], ref.at[g], sems.at[n, g])
        for n, (hbm, ref) in enumerate(zip(refs[:count], refs[count:-1]))
        for g in range(ref.shape[0])
    ]
    for copy in copies:
        copy.start()
    for copy in copies:
        copy.wait()


def load(order, place, ranks, first, group, *factors):
    outs = [jax.ShapeDtypeStruct((group,) + x.shape[1:], x.dtype) for x in factors]
    return order.call(
        functools.partial(load_kernel, first=first),
        outs,
        (place, ranks, *factors),
        [SMEM_SPEC, SMEM_SPEC] + [HBM_SPEC] * len(factors),
        [VMEM_SPEC] * len(factors),
        scratch=[pltpu.SemaphoreType.DMA((len(factors), group))],
        estimate=pl.CostEstimate(flops=0, bytes_accessed=sum(4 * x.size for x in outs), transcendentals=0),
    )


def small(kernel, outs, *args, scalars=0, order=None):
    in_specs = [SMEM_SPEC] * scalars + [VMEM_SPEC] * (len(args) - scalars)
    out_specs = [VMEM_SPEC] * len(outs)
    outs = [jax.ShapeDtypeStruct(shape, dtype) for shape, dtype in outs]
    if order is not None:
        return order.call(kernel, outs, args, in_specs, out_specs)
    return pl.pallas_call(
        kernel,
        out_shape=outs,
        in_specs=in_specs,
        out_specs=out_specs,
        compiler_params=pltpu.CompilerParams(vmem_limit_bytes=SMALL_VMEM),
    )(*args)


def small_result(order, kernel, whole, result, others, *args, scalars=0):
    group, shape, dtype = whole
    begun = [] if result is None else [result]
    return order.call(
        kernel,
        [jax.ShapeDtypeStruct(shape, dtype)] + [jax.ShapeDtypeStruct(*other) for other in others],
        (*args, *begun),
        [SMEM_SPEC] * scalars + [VMEM_SPEC] * (len(args) - scalars) + [HBM_SPEC] * len(begun),
        [HBM_SPEC] + [VMEM_SPEC] * len(others),
        scratch=[pltpu.VMEM((group,) + shape[1:], dtype), pltpu.SemaphoreType.DMA],
        aliases={len(args): 0} if begun else None,
    )


def keep(part_ref, whole_ref, sem, first):
    copy = pltpu.make_async_copy(part_ref, whole_ref.at[pl.ds(first, part_ref.shape[0])], sem)
    copy.start()
    return copy


def stack_kernel(*refs):
    for member, ref in enumerate(refs[:-1]):
        refs[-1][:, member] = ref[...]


def misfit_of(own_ref, fore_ref, back_ref, observed_ref, first):
    observed = observed_ref[pl.ds(first, own_ref.shape[0])]
    return own_ref[...] + fore_ref[...].astype(F32) + back_ref[...].astype(F32) - observed


def misfit_kernel(own_ref, fore_ref, back_ref, observed_ref, half_ref, *, first):
    half_ref[...] = misfit_of(own_ref, fore_ref, back_ref, observed_ref, first).astype(BF16)


def misfit_last_kernel(own_ref, fore_ref, back_ref, observed_ref, *rest, first):
    out_ref, half_ref, part_ref, sem = rest[-4:]
    misfit = misfit_of(own_ref, fore_ref, back_ref, observed_ref, first)
    part_ref[...] = misfit
    copy = keep(part_ref, out_ref, sem, first)
    half_ref[...] = misfit.astype(BF16)
    copy.wait()


def after_kernel(token_ref, ref, out_ref):
    out_ref[...] = ref[...]


def add_kernel(own_ref, received_ref, sum_ref, *, at):
    if received_ref.shape[1] < own_ref.shape[1]:
        sum_ref[...] = own_ref[...].astype(BF16)
    rows = pl.ds(at, received_ref.shape[1])
    sum_ref[:, rows, :] = (own_ref[:, rows, :] + received_ref[...].astype(F32)).astype(BF16)


def add(own, received, at=0):
    return small(functools.partial(add_kernel, at=at), [(own.shape, BF16)], own, received)[0]


def part_of(place, total_ref, chip_flip, core_flip):
    member = place[place.shape[0] - 1] ^ (2 * chip_flip + core_flip)
    count = total_ref.shape[1] // 4
    return total_ref[:, pl.ds(member * count, count), :]


def outward_kernel(place, total_ref, far_ref, near_ref):
    far_ref[...] = part_of(place, total_ref, 1, 1).astype(BF16)
    near_ref[...] = part_of(place, total_ref, 0, 1).astype(BF16)


def across_kernel(place, total_ref, received_ref, out_ref):
    out_ref[...] = (part_of(place, total_ref, 1, 0) + received_ref[...].astype(F32)).astype(BF16)


def step_down(place, step, total_ref, near_ref, other_ref, model_ref, new_ref, first, model_first):
    total = part_of(place, total_ref, 0, 0) + near_ref[...].astype(F32) + other_ref[...].astype(F32)
    for g in range(total.shape[0]):
        new_ref[g] = model_ref[model_first + g] - step[first + g] * total[g]


def model_kernel(place, step, total_ref, near_ref, other_ref, model_ref, new_ref, half_ref, *, first, model_first):
    step_down(place, step, total_ref, near_ref, other_ref, model_ref, new_ref, first, model_first)
    half_ref[...] = new_ref[...].astype(BF16)


def model_last_kernel(place, step, total_ref, near_ref, other_ref, model_ref, *rest, first, model_first):
    out_ref, part_ref, sem = rest[-3:]
    step_down(place, step, total_ref, near_ref, other_ref, model_ref, part_ref, first, model_first)
    keep(part_ref, out_ref, sem, first).wait()


def ring_order(count):
    return [2 * k for k in range(count // 2)] + [2 * k + 1 for k in reversed(range(count // 2))]


class Rings:
    def __init__(self, col_count):
        self.count = col_count
        order = ring_order(col_count)
        self.fore = [(order[k], order[(k + 1) % col_count]) for k in range(col_count)]
        self.back = [(b, a) for a, b in self.fore]
        ahead_of = [[order[(order.index(c) + k) % col_count] for k in range(col_count)] for c in range(col_count)]
        mine = lax.dynamic_slice(jnp.array(ahead_of, jnp.int32), (lax.axis_index("col"), 0), (1, col_count))
        self.table = jnp.concatenate([mine[0], lax.axis_index("row").astype(jnp.int32)[None]])

    def ahead(self, x):
        return lax.ppermute(x, "col", self.fore)

    def behind(self, x):
        return lax.ppermute(x, "col", self.back)


def swap_core(x):
    return lax.ppermute(x, "row", [(k, k ^ 1) for k in range(4)])


def swap_chip(x):
    return lax.ppermute(x, "row", [(k, k ^ 2) for k in range(4)])


def after(token, x):
    return small(after_kernel, [(x.shape, x.dtype)], token, x)[0]


def gather_model(half, token=None):
    across = swap_chip(half)
    beside = swap_core(half)
    if token is not None:
        across = after(token, across)
    corner = swap_core(across)
    group, count, lines = half.shape
    return small(stack_kernel, [((group, 4, count, lines), BF16)], half, beside, across, corner)[0]


class Results:
    model = None
    misfit = None


def flow(order, rings, results, factors, ranks, model_init, observed, step, first, group, token):
    u, v = factors[first]
    size = u.shape[2]
    rows = u.shape[1] // rings.count
    far = rings.count // 2
    cut = rows * size // 2
    place = rings.table
    model, model_first = model_init, first
    half = model_init[first : first + group].astype(BF16)
    for sweep in range(ITERS):
        final = sweep == ITERS - 1
        x = gather_model(half, None if sweep else token)
        fore, back = forward(order, u, v, x, ranks, place, (far,), first, rows, BF16, 2)
        fore, back = rings.ahead(fore), rings.behind(back)
        yield
        for k in range(far - 1, 0, -1):
            up, down = forward(order, u, v, x, ranks, place, (k, -k), first, rows, F32)
            fore = rings.ahead(add(up, fore))
            back = rings.behind(add(down, back, cut if k == far - 1 else 0))
            yield
        (own,) = forward(order, u, v, x, ranks, place, (0,), first, rows, F32)
        args = (own, fore, back, observed)
        if final:
            kernel = functools.partial(misfit_last_kernel, first=first)
            whole = (group, observed.shape, F32)
            results.misfit, half = small_result(order, kernel, whole, results.misfit, [(own.shape, BF16)], *args)
        else:
            (half,) = small(functools.partial(misfit_kernel, first=first), [(own.shape, BF16)], *args, order=order)
        fore, back = rings.ahead(half), rings.behind(half)
        yield
        total = adjoint(order, u, v, [half], ranks, None, place, (0,), first, rows)
        yield
        for k in range(1, far):
            arrived = [fore, back]
            if k < far - 1:
                fore, back = rings.ahead(fore), rings.behind(back)
            else:
                fore, back = rings.ahead(fore[:, :cut]), rings.behind(back[:, cut:])
            total = adjoint(order, u, v, arrived, ranks, total, place, (-k, k), first, rows)
            yield
        total = adjoint(order, u, v, [fore, back], ranks, total, place, (far,), first, rows)
        lines = total.shape[2]
        count = total.shape[1] // 4
        part = ((group, count, lines), BF16)
        out, near = small(outward_kernel, [part, part], place, total, scalars=1, order=order)
        out, near = swap_core(out), swap_core(near)
        yield
        (out,) = small(across_kernel, [part], place, total, out, scalars=1, order=order)
        out = swap_chip(out)
        yield
        args = (place, step, total, near, out, model)
        told = dict(first=first, model_first=model_first)
        if final:
            whole = (group, (step.shape[0], count, lines), F32)
            kernel = functools.partial(model_last_kernel, **told)
            (results.model,) = small_result(order, kernel, whole, results.model, [], *args, scalars=2)
        else:
            outs = [((group, count, lines), F32), part]
            kernel = functools.partial(model_kernel, **told)
            model, half = small(kernel, outs, *args, scalars=2, order=order)
            model_first = 0
        yield


def local_ring(u, v, ranks, model_init, observed, step, *, col_count):
    frequencies = u.shape[0]
    rings = Rings(col_count)
    group = frequencies // GROUPS
    firsts = range(0, frequencies, group)
    order, results = Order(jnp.zeros((8, 128), F32)), Results()
    factors = {0: load(order, rings.table, ranks, 0, group, u, v)}
    tokens = [order.token] + [None] * (GROUPS - 1)
    flows = [
        flow(order, rings, results, factors, ranks, model_init, observed, step, first, group, token)
        for first, token in zip(firsts, tokens)
    ]
    waits = [LAG * n for n in range(GROUPS)]
    running = [True] * GROUPS
    turn = 0
    while any(running):
        for n in range(1, GROUPS):
            if turn == LAG * n - 2:
                early = load(order, rings.table, ranks, firsts[n], group, v)
            if turn == LAG * n:
                factors[firsts[n]] = load(order, rings.table, ranks, firsts[n], group, u) + early
        turn += 1
        for n, work in enumerate(flows):
            if waits[n] > 0:
                waits[n] -= 1
            elif running[n]:
                running[n] = next(work, work) is not work
    return (results.model, results.misfit)


def solution(mesh):
    col_count, row_count = mesh.shape["col"], mesh.shape["row"]

    def local(u, v, ranks, model_init, observed, step):
        if row_count == 4 and col_count % 2 == 0 and col_count >= 4 and u.shape[1] % (2 * col_count) == 0:
            return local_ring(u, v, ranks, model_init, observed, step, col_count=col_count)
        return local_plain(u, v, ranks, model_init, observed, step)

    return jax.shard_map(
        local,
        mesh=mesh,
        in_specs=(
            P(None, "row", None, "col", None),
            P(None, "row", None, "col", None),
            P(None, "row", "col"),
            P(None, ("col", "row"), None),
            P(None, ("row", "col"), None),
            P(),
        ),
        out_specs=(P(None, ("col", "row"), None), P(None, ("row", "col"), None)),
        check_vma=False,
    )
```
